128 devices in a mesh: grp: 8 (over x, core), sub: 16 (over y, z).
Axes of the slice: x: 4, y: 4, z: 4, core: 2. Of those that a mesh axis runs over, the one named last changes fastest.
Arguments:
- points: float32 [3, 2097152], P(None, ('grp', 'sub'))
- forces: float32 [3, 2097152], P(None, ('grp', 'sub')), may hold values from -6 to 6
- counts: int32 [32768], P(('grp', 'sub')), may hold values from 1 to 64, as said below
- droplet: int32 [2097152], P(('grp', 'sub')), may hold values from 0 to 255
- contrast: float32 [256], replicated, may hold values from 0.1 to 10
- ulist: int32 [32768, 27], P(('grp', 'sub')), may hold values from -1 to 32767, as said below
- vlist0: int32 [32768, 40], P(('grp', 'sub')), may hold values from -1 to 32767, as said below
- vlist1: int32 [4096, 40], P(('grp', 'sub')), may hold values from -1 to 4095, as said below
- vlist2: int32 [512, 40], P(('grp', 'sub')), may hold values from -1 to 511, as said below
- wave: float32 [3, 296], replicated, may hold values from -6 to 6
- phases: float32 [2, 296], replicated, may hold values from -3.140625 to 3.140625
- p2m_mix: float32 [3, 296], replicated, may hold values from -0.4375 to 0.4375
- m2m: bfloat16 [8, 296, 296], replicated, may hold values from -0.125 to 0.125
- m2l: bfloat16 [40, 296, 296], replicated, may hold values from -0.0546875 to 0.0546875
- l2l: bfloat16 [8, 296, 296], replicated, may hold values from -0.25 to 0.25
- l2p_mix: float32 [3, 296], replicated, may hold values from -0.375 to 0.375
Outputs:
- velocity: float32 [3, 2097152], P(None, ('grp', 'sub'))
The draws below stay inside these ranges and needn't reach their ends.
Inputs may be any that keep to these rules, and one draw needn't show every extreme that they name: `counts`: every leaf holds at least one point; the first leaf of each run of 256 leaves holds 64. `ulist`: each entry is -1 or a leaf at most 16 places from its leaf in Morton order; the first entry is the leaf itself, the second and third are the leaves 16 places before and after it where those exist. Entries may repeat. `vlist0`: each entry is -1 or a leaf of the same run of 4096 leaves as its own leaf. The first entry is the leaf 4096 // 2 places further in Morton order, counted round within that run; every other entry is -1 or a child of a neighbour of its parent that is not adjacent to it. Entries may repeat. `vlist1`: the first entry is the octant 4096 // 2 places further in Morton order, counted round within the level; every other entry is -1 or a child of a neighbour of the octant's parent, not adjacent to the octant. Entries may repeat. `vlist2`: the first entry is the octant 512 // 2 places further in Morton order, counted round within the level; every other entry is -1 or a child of a neighbour of the octant's parent, not adjacent to the octant. Entries may repeat.
All inputs are finite; a program needn't handle non-finite values.
Results may differ from the reference program's by a relative error of at most 0.00057.
Values may be sent and summed in bfloat16 or wider, within the bound.
No kernel may reach another device: no remote copies, remote signals or barrier semaphores. Data moves between devices by JAX's collectives and lax.ppermute only.
A program may use at most 192 MiB of HBM per device.

```python
import math
import jax
import jax.numpy as jnp
from jax import lax

LEAF_DEV = 256
PTS = 64
NC = 296
VEC = 40
NU = 27
HALO = 16
NDROP = 256
NLEAF = 32768
GROUP_LEAVES = 4096
N1 = 4096
N2 = 512
POINTS = 2097152


def leaf_center_drawn(leaf_index):
    coords = []
    for dim_index in range(3):
        coord_value = jnp.zeros_like(leaf_index)
        for bit_index in range(10):
            coord_value = coord_value + ((leaf_index >> 3 * bit_index + dim_index & 1) << bit_index)
        coords.append(coord_value.astype(jnp.float32) + 0.5)
    return jnp.stack(coords)


def morton_coords(index):
    coords = []
    for dim_index in range(3):
        coord_value = jnp.zeros_like(index)
        for bit_index in range(10):
            coord_value = coord_value + ((index >> 3 * bit_index + dim_index & 1) << bit_index)
        coords.append(coord_value)
    return coords


def morton_code(coords):
    code_value = jnp.zeros_like(coords[0])
    for dim_index in range(3):
        for bit_index in range(10):
            code_value = code_value + ((coords[dim_index] >> bit_index & 1) << 3 * bit_index + dim_index)
    return code_value


def interaction_entries(key, count, slots, group):
    own_index = jnp.arange(count, dtype=jnp.int32)[:, None]
    own_coords = morton_coords(own_index)
    pick = jax.random.randint(key, (count, slots), 0, 216)
    steps_list = [pick % 6, pick // 6 % 6, pick // 36]
    valid = jnp.ones((count, slots), dtype=bool)
    near = jnp.ones((count, slots), dtype=bool)
    targets = []
    for dim_index in range(3):
        target = 2 * (own_coords[dim_index] >> 1) + steps_list[dim_index] - 2
        valid = valid & (target >= 0) & (target < 1024)
        near = near & (jnp.abs(target - own_coords[dim_index]) <= 1)
        targets.append(jnp.clip(target, 0, 1023))
    code_value = morton_code(targets)
    valid = valid & ~near & (code_value < count) & (code_value // group == own_index // group)
    entries = jnp.where(valid, code_value, -1)
    within = own_index % group
    mirror = own_index - within + (within + group // 2) % group
    column = jnp.arange(slots, dtype=jnp.int32)[None, :]
    entries = jnp.where(column == 0, mirror, entries)
    return entries.astype(jnp.int32)


def draw_points(key, part):
    key = jax.random.fold_in(key, 11)
    leaf_index = jnp.arange(NLEAF, dtype=jnp.int32)
    centers = jnp.repeat(leaf_center_drawn(leaf_index), PTS, axis=1)
    spread = jax.random.uniform(key, (3, POINTS), jnp.float32, -0.5, 0.5)
    return centers + spread


def draw_counts(key, part):
    key = jax.random.fold_in(key, 12)
    first_key, second_key = jax.random.split(key)
    first_factor = jax.random.randint(first_key, (NLEAF,), 0, PTS)
    second_factor = jax.random.randint(second_key, (NLEAF,), 0, PTS)
    counted = 1 + first_factor * second_factor // PTS
    leaf_index = jnp.arange(NLEAF, dtype=jnp.int32)
    return jnp.where(leaf_index % LEAF_DEV == 0, PTS, counted).astype(jnp.int32)


def draw_ulist(key, part):
    key = jax.random.fold_in(key, 13)
    first_key, second_key = jax.random.split(key)
    leaf_index = jnp.arange(NLEAF, dtype=jnp.int32)[:, None]
    shifted = jax.random.randint(first_key, (NLEAF, NU), -HALO, HALO + 1)
    column = jnp.arange(NU, dtype=jnp.int32)[None, :]
    shifted = jnp.where(column == 0, 0, shifted)
    shifted = jnp.where(column == 1, -HALO, shifted)
    shifted = jnp.where(column == 2, HALO, shifted)
    chosen = jnp.clip(leaf_index + shifted, 0, NLEAF - 1)
    dropped = (jax.random.randint(second_key, (NLEAF, NU), 0, 4) == 0) & (column >= 3)
    return jnp.where(dropped, -1, chosen).astype(jnp.int32)


def draw_vlist0(key, part):
    key = jax.random.fold_in(key, 14)
    return interaction_entries(key, NLEAF, VEC, GROUP_LEAVES)


def draw_vlist1(key, part):
    key = jax.random.fold_in(key, 15)
    return interaction_entries(key, N1, VEC, N1)


def draw_vlist2(key, part):
    key = jax.random.fold_in(key, 16)
    return interaction_entries(key, N2, VEC, N2)


def with_ends(values, stream_key, smallest, largest):
    spot = [jax.random.randint(jax.random.fold_in(stream_key, axis), (), 0, length) for axis, length in enumerate(values.shape)]
    longest = values.shape.index(max(values.shape))
    next_to = spot[:longest] + [(spot[longest] + 1) % values.shape[longest]] + spot[longest + 1:]
    return values.at[tuple(spot)].set(smallest).at[tuple(next_to)].set(largest)


def block_levels(stream_key, extent, cuts, low, largest):
    loudness = 1.0
    for dim, shards_of in cuts:
        steps = jax.random.uniform(jax.random.fold_in(jax.random.fold_in(stream_key, 6), dim), (shards_of,), jnp.float32, low / len(cuts), largest / len(cuts))
        loudness = loudness * jnp.repeat(jnp.exp(steps), extent[dim] // shards_of).reshape((-1,) + (1,) * (len(extent) - 1 - dim))
    return loudness


def normal_values(rng, shape, width, most, cuts=(), kind=jnp.bfloat16):
    drawn = jax.random.normal(rng, shape, jnp.float32) * width
    if len(cuts) > 0:
        drawn = block_levels(rng, shape, cuts, -0.22, 0.18) * drawn
    return jnp.clip(drawn, min=-most, max=most).astype(kind)


def setup_inputs(seed: int = 0) -> dict:
    arg_keys = jax.random.split(jax.random.key(seed), 17)
    return {
        "points": draw_points(jax.random.fold_in(arg_keys[16], 71), 0),
        "forces": normal_values(arg_keys[1], (3, POINTS), 1.0, 6.0, ((1, 128),), jnp.float32),
        "counts": draw_counts(jax.random.fold_in(arg_keys[16], 71), 0),
        "droplet": with_ends(jax.random.randint(arg_keys[3], (POINTS,), 0, NDROP), jax.random.fold_in(arg_keys[3], 1), 0, NDROP - 1).astype(jnp.int32),
        "contrast": jnp.clip(jnp.exp(jax.random.uniform(arg_keys[4], (NDROP,), jnp.float32, math.log(0.1), math.log(10.0))), 0.1, 10.0),
        "ulist": draw_ulist(jax.random.fold_in(arg_keys[16], 71), 0),
        "vlist0": draw_vlist0(jax.random.fold_in(arg_keys[16], 71), 0),
        "vlist1": draw_vlist1(jax.random.fold_in(arg_keys[16], 71), 0),
        "vlist2": draw_vlist2(jax.random.fold_in(arg_keys[16], 71), 0),
        "wave": normal_values(arg_keys[9], (3, NC), 1.5, 6.0, (), jnp.float32),
        "phases": jnp.clip(jax.random.uniform(arg_keys[10], (2, NC), jnp.float32, -3.140625, 3.140625), -3.140625, 3.140625),
        "p2m_mix": normal_values(arg_keys[11], (3, NC), (3 * PTS) ** -0.5, 0.4375, (), jnp.float32),
        "m2m": normal_values(arg_keys[12], (8, NC, NC), (8 * NC) ** -0.5, 0.125),
        "m2l": normal_values(arg_keys[13], (VEC, NC, NC), (VEC * NC) ** -0.5, 0.0546875),
        "l2l": normal_values(arg_keys[14], (8, NC, NC), (2 * NC) ** -0.5, 0.25),
        "l2p_mix": normal_values(arg_keys[15], (3, NC), NC ** -0.5, 0.375, (), jnp.float32),
    }


EPS_REG = 0.3


def leaf_center(leaf_index):
    coords = []
    for dim_index in range(3):
        coord_value = jnp.zeros_like(leaf_index)
        for bit_index in range(10):
            coord_value = coord_value + (((leaf_index >> (3 * bit_index + dim_index)) & 1) << bit_index)
        coords.append(coord_value.astype(jnp.float32) + 0.5)
    return jnp.stack(coords)


def point_mask(counts, slots):
    slot_index = jnp.arange(slots, dtype=jnp.int32)
    return (slot_index[None, :] < counts[:, None]).reshape(-1).astype(jnp.float32)


def multipoles(offsets, masked, wave, phases, p2m_mix, slots):
    phase_arg = jnp.dot(wave.T, offsets, precision=lax.Precision.HIGHEST) + phases[0][:, None]
    charge = jnp.dot(p2m_mix.T, masked, precision=lax.Precision.HIGHEST)
    weighted = (charge * jnp.cos(phase_arg)).reshape(wave.shape[1], -1, slots).sum(-1)
    return weighted.T.astype(jnp.bfloat16)


def upward(children, m2m):
    coeffs = m2m.shape[2]
    count_rows = children.shape[0] // 8
    grouped = children.reshape(count_rows, 8 * coeffs)
    return jnp.dot(grouped, m2m.reshape(8 * coeffs, coeffs), preferred_element_type=jnp.float32).astype(jnp.bfloat16)


def apply_m2l(source_rows, m2l, scale):
    count_rows = source_rows.shape[0]
    coeffs = m2l.shape[2]
    return jnp.dot(source_rows.reshape(count_rows, -1), m2l.reshape(-1, coeffs), preferred_element_type=jnp.float32) * scale


def translate(sources, vlist, group_base, m2l, scale):
    position = vlist - group_base
    present = (vlist >= 0).astype(jnp.bfloat16)
    source_rows = jnp.take(sources, jnp.clip(position, 0, sources.shape[0] - 1), axis=0)
    return apply_m2l(source_rows * present[..., None], m2l, scale)


def downward(parent_local, l2l):
    coeffs = l2l.shape[2]
    parent_bf = parent_local.astype(jnp.bfloat16)
    operator = l2l.transpose(1, 0, 2).reshape(coeffs, 8 * coeffs)
    children = jnp.dot(parent_bf, operator, preferred_element_type=jnp.float32)
    return children.reshape(parent_local.shape[0] * 8, coeffs)


def evaluate_far(offsets, leaf_local, wave, phases, l2p_mix, slots):
    phase_arg = jnp.dot(wave.T, offsets, precision=lax.Precision.HIGHEST) + phases[1][:, None]
    spread = jnp.repeat(leaf_local.T, slots, axis=1)
    return jnp.dot(l2p_mix, spread * jnp.cos(phase_arg), precision=lax.Precision.HIGHEST)


def near_field(targets, extended, uindex, upresent, slots):
    leaf_count = uindex.shape[0]
    ext_leaves = extended.shape[1] // slots
    near_count = uindex.shape[1]
    source_leaf = extended.reshape(6, ext_leaves, slots).transpose(1, 0, 2)
    target_leaf = targets.reshape(3, leaf_count, slots).transpose(1, 0, 2)
    tile_size = 16
    tiles = leaf_count // tile_size
    eps_sq = EPS_REG * EPS_REG

    def tile_velocity(operands):
        tile_targets, tile_index, tile_present = operands
        sources = jnp.take(source_leaf, jnp.clip(tile_index, 0, ext_leaves - 1), axis=0)
        sources = sources * tile_present[..., None, None]
        sources = sources.transpose(0, 2, 1, 3).reshape(tile_size, 6, near_count * slots)
        separation = tile_targets[:, :, :, None] - sources[:, 0:3, None, :]
        force = sources[:, 3:6]
        dist_sq = jnp.sum(separation * separation, axis=1) + eps_sq
        inv_cube = dist_sq ** -1.5
        projected = jnp.sum(separation * force[:, :, None, :], axis=1)
        velocity = ((dist_sq + eps_sq) * inv_cube)[:, None] * force[:, :, None, :] + separation * (projected * inv_cube)[:, None]
        return velocity.sum(-1) / (8.0 * math.pi)

    result = lax.map(tile_velocity, (target_leaf.reshape(tiles, tile_size, 3, slots), uindex.reshape(tiles, tile_size, near_count), upresent.astype(jnp.float32).reshape(tiles, tile_size, near_count)))
    return result.reshape(leaf_count, 3, slots).transpose(1, 0, 2).reshape(3, leaf_count * slots)


def reference(points, forces, counts, droplet, contrast, ulist, vlist0, vlist1, vlist2, wave, phases, p2m_mix, m2m, m2l, l2l, l2p_mix):
    leaf_count = counts.shape[0]
    block_count = leaf_count // LEAF_DEV
    block_slots = LEAF_DEV * PTS
    leaf_ids = jnp.arange(leaf_count, dtype=jnp.int32)
    alive_mask = point_mask(counts, PTS)
    masked = forces * alive_mask[None, :]
    offsets = points - jnp.repeat(leaf_center(leaf_ids), PTS, axis=1)
    offset_blocks = offsets.reshape(3, block_count, block_slots).transpose(1, 0, 2)
    masked_blocks = masked.reshape(3, block_count, block_slots).transpose(1, 0, 2)
    leaf_mult = lax.map(lambda pair: multipoles(pair[0], pair[1], wave, phases, p2m_mix, PTS), (offset_blocks, masked_blocks)).reshape(leaf_count, -1)
    parent_mult = upward(leaf_mult, m2m)
    grand_mult = upward(parent_mult, m2m)
    grand_local = translate(grand_mult, vlist2, 0, m2l, 0.25)
    parent_local = downward(grand_local, l2l) + translate(parent_mult, vlist1, 0, m2l, 0.5)
    leaf_terms = lax.map(lambda block_list: translate(leaf_mult, block_list, 0, m2l, 1.0), vlist0.reshape(block_count, LEAF_DEV, -1)).reshape(leaf_count, -1)
    leaf_local = downward(parent_local, l2l) + leaf_terms
    local_blocks = leaf_local.reshape(block_count, LEAF_DEV, -1)
    far_blocks = lax.map(lambda pair: evaluate_far(pair[0], pair[1], wave, phases, l2p_mix, PTS), (offset_blocks, local_blocks))
    far_velocity = far_blocks.transpose(1, 0, 2).reshape(3, -1)
    extended = jnp.concatenate([points, masked], axis=0)
    near_velocity = near_field(points, extended, ulist, ulist >= 0, PTS)
    factor = 2.0 / (1.0 + contrast[droplet])
    return factor[None, :] * (near_velocity + far_velocity) * alive_mask[None, :]
```

```python
import functools
import math

import jax
import jax.numpy as jnp
from jax import lax
from jax.experimental import pallas as pl
from jax.experimental.pallas import tpu as pltpu
from jax.sharding import PartitionSpec as P

PTS = 64
HALO = 16
EPS_SQ = 0.3 * 0.3
LANES = 128
NEIGHBOURS = 27
ROOT_BITS = 5

F32 = jnp.float32
BF16 = jnp.bfloat16

COS_COEFFS = (
    0.9999999890590235,
    -19.739204499453994,
    64.93911745989843,
    -85.45013953092186,
    60.167630951185615,
    -25.967599249120923,
    6.528658161956132,
)

NT = (((1,), (1,)), ((), ()))
NN = (((1,), (0,)), ((), ()))


def params(megabytes):
    return pltpu.CompilerParams(vmem_limit_bytes=megabytes * 1024 * 1024)


def dot(left, right, dims=NN):
    return lax.dot_general(left, right, dims, preferred_element_type=F32)


def split3(value):
    high = lax.reduce_precision(value, 8, 7)
    rest = value - high
    middle = lax.reduce_precision(rest, 8, 7)
    return high, middle, rest - middle


def kernel_split3(value):
    high = value.astype(BF16).astype(F32)
    rest = value - high
    middle = rest.astype(BF16).astype(F32)
    return high, middle, rest - middle


def kernel_split2(value):
    high = value.astype(BF16)
    return high, (value - high.astype(F32)).astype(BF16)


def weight_rows(matrix, first_row, bias=None):
    coeffs = matrix.shape[1]
    high, middle, low = split3(matrix)
    groups = []
    for piece in (high, high, middle, middle, high, low):
        groups.append(jnp.pad(piece, ((first_row, 5 - first_row), (0, 0))))
    if bias is None:
        groups.append(jnp.zeros((8, coeffs), F32))
    else:
        groups.append(jnp.pad(jnp.stack(split3(bias)), ((0, 5), (0, 0))))
    groups.append(jnp.zeros((8, coeffs), F32))
    return jnp.concatenate(groups, axis=0).T.astype(BF16)


def feature_pieces(rows):
    high, middle, low = kernel_split3(rows)
    ones = jnp.where(lax.broadcasted_iota(jnp.int32, rows.shape, 0) < 3, 1.0, 0.0)
    pieces = [high, middle, high, middle, low, high, ones, jnp.zeros_like(rows)]
    return jnp.concatenate(pieces, axis=0).astype(BF16)


def cos_turns(turns):
    part = turns - jnp.round(turns)
    square = part * part
    value = jnp.full_like(square, COS_COEFFS[-1])
    for coeff in COS_COEFFS[-2::-1]:
        value = value * square + coeff
    return value


def center_rows(ids):
    axis = lax.broadcasted_iota(jnp.int32, ids.shape, 0)
    total = jnp.zeros_like(ids)
    for bit in range(ROOT_BITS):
        total = total + (((ids >> (axis + 3 * bit)) & 1) << bit)
    return total.astype(F32) + 0.5


def block_features(block):
    row = lax.broadcasted_iota(jnp.int32, block.shape, 0)
    ids = block[7:8, :].astype(jnp.int32)
    centers = center_rows(jnp.broadcast_to(jnp.maximum(ids, 0), block.shape))
    rows = jnp.where(row < 3, block - centers, jnp.where(row < 6, block, 0.0))
    return rows, ids


def pack_leaves(read_pair, count_of, pairs, dest, start, current):
    lane = lax.broadcasted_iota(jnp.int32, (8, LANES), 1)

    def body(pair, carry):
        offset, held = carry
        value = read_pair(pair)
        for half in range(2):
            count = count_of(2 * pair + half)
            block, place = offset >> 7, offset & 127
            rolled = pltpu.roll(value, (place + 64 * half) & 127, 1)
            merged = jnp.where(lane >= place, rolled, held)
            dest[block] = merged
            held = jnp.where(place + count >= LANES, rolled, merged)
            offset = offset + count
        return offset, held

    offset, held = lax.fori_loop(0, pairs, body, (start, current))
    dest[offset >> 7] = held
    return offset


def finish_pack(dest, end):
    lane = lax.broadcasted_iota(jnp.int32, (8, LANES), 1)
    row = lax.broadcasted_iota(jnp.int32, (8, LANES), 0)
    block, place = end >> 7, end & 127
    empty = jnp.where(row == 7, -1.0, 0.0)
    dest[block] = jnp.where(lane >= place, empty, dest[block])


def upward_kernel(coeffs, base_ref, counts_ref, slots_ref, weights_ref, m2m_ref,
                  packed_ref, leaf_ref, up_ref, acc, staged, parents):
    leaves = counts_ref.shape[0]
    lane = lax.broadcasted_iota(jnp.int32, (8, LANES), 1)

    def read_pair(pair):
        return slots_ref[:, pl.ds(pl.multiple_of(pair * LANES, LANES), LANES)]

    total = pack_leaves(
        read_pair, lambda leaf: counts_ref[leaf], leaves // 2, packed_ref,
        jnp.int32(0), jnp.zeros((8, LANES), F32),
    )
    finish_pack(packed_ref, total)
    acc[...] = jnp.zeros_like(acc)
    first = base_ref[0]

    def body(block, carry):
        rows, ids = block_features(packed_ref[block])
        both = dot(weights_ref[...], feature_pieces(rows))
        part = cos_turns(both[:coeffs]) * both[coeffs:]
        high, low = kernel_split2(part)
        local = jnp.broadcast_to(ids - first, (leaves, LANES))
        which = jnp.where(lax.broadcasted_iota(jnp.int32, (leaves, LANES), 0) == local, 1.0, 0.0).astype(BF16)
        acc[...] += dot(
            jnp.concatenate([which, which], axis=1), jnp.concatenate([high, low], axis=1), NT
        )
        return carry

    lax.fori_loop(0, (total + LANES - 1) >> 7, body, 0)
    leaf = acc[...].astype(BF16)
    leaf_ref[...] = leaf
    leaf_f32 = leaf.astype(F32)
    tiles = staged.shape[0]

    def stage(target, value):
        for tile in range(tiles):
            low_col = tile * LANES
            width = min(LANES, coeffs - low_col)
            target[tile, :, :width] = value[:, low_col:low_col + width]

    def child(source, which, rows):
        parts = [source[tile, pl.ds(which, rows, stride=8), :] for tile in range(tiles)]
        return jnp.concatenate(parts, axis=1)[:, :coeffs].astype(BF16)

    stage(staged, leaf_f32)
    above = jnp.zeros((leaves // 8, coeffs), F32)
    for which in range(8):
        above = above + dot(child(staged, which, leaves // 8), m2m_ref[which])
    up = above.astype(BF16)
    stage(parents, up.astype(F32))
    top = jnp.zeros((leaves // 64, coeffs), F32)
    for which in range(8):
        top = top + dot(child(parents, which, leaves // 64), m2m_ref[which])
    up_ref[0:leaves // 8, :] = up
    pad = jnp.zeros((up_ref.shape[0] - leaves // 8 - leaves // 64, coeffs), F32)
    up_ref[leaves // 8:, :] = jnp.concatenate([top, pad], axis=0).astype(BF16)


def upward_pass(first_leaf, counts, slots, weights, m2m):
    leaves, coeffs = counts.shape[0], m2m.shape[1]
    blocks = slots.shape[1] // LANES
    tiles = -(-coeffs // LANES)
    smem = pl.BlockSpec(memory_space=pltpu.SMEM)
    vmem = pl.BlockSpec(memory_space=pltpu.VMEM)
    up_rows = -(-(leaves // 8 + leaves // 64) // 16) * 16
    return pl.pallas_call(
        functools.partial(upward_kernel, coeffs),
        out_shape=(
            jax.ShapeDtypeStruct((blocks + 2, 8, LANES), F32),
            jax.ShapeDtypeStruct((leaves, coeffs), BF16),
            jax.ShapeDtypeStruct((up_rows, coeffs), BF16),
        ),
        in_specs=[smem, smem, vmem, vmem, vmem],
        out_specs=(vmem, vmem, vmem),
        scratch_shapes=[
            pltpu.VMEM((leaves, coeffs), F32),
            pltpu.VMEM((tiles, leaves, LANES), F32),
            pltpu.VMEM((tiles, leaves // 8, LANES), F32),
        ],
        compiler_params=params(32),
        name="upward",
    )(first_leaf, counts, slots, weights, m2m)


def near_kernel(base_ref, counts_ref, left_counts, right_counts, packed_ref, left_ref, right_ref,
                ulist_ref, near_ref, sources, which_source, lists, shares, targets, acc, starts):
    leaves = counts_ref.shape[0]
    window = leaves + 2 * HALO
    halo_blocks = HALO * PTS // LANES
    first = base_ref[0]
    lane = lax.broadcasted_iota(jnp.int32, (8, LANES), 1)
    row = lax.broadcasted_iota(jnp.int32, (8, LANES), 0)
    empty = jnp.where(row == 7, -1.0, 0.0)

    left_total = jnp.int32(0)
    for leaf in range(HALO):
        left_total = left_total + left_counts[leaf]
    left_start = HALO * PTS - left_total

    def note_left(leaf, offset):
        starts[leaf] = offset
        return offset + left_counts[leaf]

    offset = lax.fori_loop(0, HALO, note_left, left_start)

    def note_own(leaf, offset):
        starts[HALO + leaf] = offset
        return offset + counts_ref[leaf]

    own_end = lax.fori_loop(0, leaves, note_own, offset)

    def note_right(leaf, offset):
        starts[HALO + leaves + leaf] = offset
        return offset + right_counts[leaf]

    end = lax.fori_loop(0, HALO, note_right, own_end)
    starts[window] = end

    def pair_of(ref):
        return lambda pair: ref[:, pl.ds(pl.multiple_of(pair * LANES, LANES), LANES)]

    pack_leaves(pair_of(left_ref), lambda leaf: left_counts[leaf], HALO // 2, sources, left_start, empty)
    own_blocks = (own_end - HALO * PTS + LANES - 1) >> 7

    def copy_block(block, carry):
        sources[halo_blocks + block] = packed_ref[block]
        return carry

    lax.fori_loop(0, own_blocks, copy_block, 0)
    held = sources[own_end >> 7]
    pack_leaves(pair_of(right_ref), lambda leaf: right_counts[leaf], HALO // 2, sources, own_end, held)
    finish_pack(sources, end)

    own_list = ulist_ref[...]
    column = lax.broadcasted_iota(jnp.int32, (leaves, window), 1)
    times = jnp.zeros((leaves, window), F32)
    for slot in range(own_list.shape[1]):
        times = times + jnp.where(own_list[:, slot:slot + 1] == column, 1.0, 0.0)
    lists[...] = times.astype(BF16)

    def mark_source(tile, carry):
        ids = sources[tile][7:8, :].astype(jnp.int32)
        local = jnp.broadcast_to(jnp.where(ids < 0, -1, ids - first + HALO), (window, LANES))
        hits = lax.broadcasted_iota(jnp.int32, (window, LANES), 0) == local
        which_source[tile] = jnp.where(hits, 1.0, 0.0).astype(BF16)
        return carry

    lax.fori_loop(left_start >> 7, (end + LANES - 1) >> 7, mark_source, 0)

    def target_block(block, carry):
        own = packed_ref[block]
        columns = jnp.transpose(
            jnp.concatenate([own, jnp.zeros((LANES - 8, LANES), F32)], axis=0)
        )
        ids = columns[:, 7:8].astype(jnp.int32) - first
        hits = lax.broadcasted_iota(jnp.int32, (LANES, leaves), 1) == ids
        row_share = dot(jnp.where(hits, 1.0, 0.0).astype(BF16), lists[...])
        shares[...] = row_share.astype(BF16)
        for axis in range(3):
            targets[axis] = jnp.broadcast_to(columns[:, axis:axis + 1], (LANES, LANES))
        acc[...] = jnp.zeros_like(acc)
        live = own[7:8, :]
        low_leaf = (jnp.min(jnp.where(live < 0.0, 1e9, live)) - first.astype(F32)).astype(jnp.int32)
        high_leaf = (jnp.max(live) - first.astype(F32)).astype(jnp.int32)
        source_low = starts[low_leaf] >> 7
        source_high = (starts[high_leaf + 2 * HALO + 1] + LANES - 1) >> 7

        def source_tile(tile, carry):
            share = dot(shares[...], which_source[tile])
            value = sources[tile]
            feature = [jnp.broadcast_to(value[k:k + 1, :], (8, LANES)) for k in range(6)]
            for chunk in range(LANES // 8):
                span = slice(8 * chunk, 8 * chunk + 8)
                dx = targets[0, span, :] - feature[0]
                dy = targets[1, span, :] - feature[1]
                dz = targets[2, span, :] - feature[2]
                dist_sq = dx * dx + dy * dy + (dz * dz + EPS_SQ)
                along = dx * feature[3] + dy * feature[4] + dz * feature[5]
                inverse = lax.rsqrt(dist_sq)
                weighted = share[span, :] * inverse
                cubed = weighted * (inverse * inverse)
                plain = weighted + EPS_SQ * cubed
                outer = along * cubed
                acc[0, span, :] += plain * feature[3] + outer * dx
                acc[1, span, :] += plain * feature[4] + outer * dy
                acc[2, span, :] += plain * feature[5] + outer * dz
            return carry

        lax.fori_loop(source_low, source_high, source_tile, 0)
        wide = lax.broadcasted_iota(jnp.int32, (LANES, LANES), 1)
        sums = jnp.zeros((LANES, LANES), F32)
        for axis in range(3):
            sums = jnp.where(wide == axis, jnp.sum(acc[axis], axis=1, keepdims=True), sums)
        near_ref[block] = jnp.transpose(sums)[0:8, :] * (1.0 / (8.0 * math.pi))
        return carry

    lax.fori_loop(0, own_blocks, target_block, 0)


def near_field(first_leaf, counts, left_counts, right_counts, packed, left, right, ulist):
    leaves = counts.shape[0]
    window = leaves + 2 * HALO
    blocks = packed.shape[0]
    source_blocks = (leaves + 2 * HALO) * PTS // LANES + 2
    smem = pl.BlockSpec(memory_space=pltpu.SMEM)
    vmem = pl.BlockSpec(memory_space=pltpu.VMEM)
    return pl.pallas_call(
        near_kernel,
        out_shape=jax.ShapeDtypeStruct((blocks, 8, LANES), F32),
        in_specs=[smem] * 4 + [vmem] * 4,
        out_specs=vmem,
        scratch_shapes=[
            pltpu.VMEM((source_blocks, 8, LANES), F32),
            pltpu.VMEM((source_blocks, window, LANES), BF16),
            pltpu.VMEM((leaves, window), BF16),
            pltpu.VMEM((LANES, window), BF16),
            pltpu.VMEM((3, LANES, LANES), F32),
            pltpu.VMEM((3, LANES, LANES), F32),
            pltpu.SMEM((window + 1,), jnp.int32),
        ],
        compiler_params=params(40),
        cost_estimate=pl.CostEstimate(flops=20_000_000_000, bytes_accessed=2_000_000, transcendentals=0),
        name="near_field",
    )(first_leaf, counts, left_counts, right_counts, packed, left, right, ulist)


def coords_of(code, bits):
    return [
        sum(((code >> (3 * bit + axis)) & 1) << bit for bit in range(bits)) for axis in range(3)
    ]


def code_of(coords, bits):
    return sum(
        ((coords[axis] >> bit) & 1) << (3 * bit + axis) for axis in range(3) for bit in range(bits)
    )


def list_places(vlist, parent_of_row, bits):
    own = coords_of(parent_of_row[:, None], bits)
    other = coords_of(vlist >> 3, bits)
    near = sum((o - m + 1) * 3 ** axis for axis, (o, m) in enumerate(zip(other, own)))
    slot = jnp.where(jnp.arange(vlist.shape[1])[None, :] == 0, NEIGHBOURS, near)
    return jnp.where(vlist >= 0, slot * 8 + (vlist & 7), -1)


def pool_blocks(parents, bits, base, extent):
    own = coords_of(parents, bits)
    columns = []
    for slot in range(NEIGHBOURS):
        steps = (slot % 3 - 1, slot // 3 % 3 - 1, slot // 9 - 1)
        columns.append(code_of([jnp.clip(m + s, 0, 2 ** bits - 1) for m, s in zip(own, steps)], bits) - base)
    columns.append((parents - base + extent // 2) % extent)
    return jnp.clip(jnp.stack(columns, axis=1), 0, extent - 1)


def far_kernel(coeffs, base_ref, counts_ref, blocks_ref, places_ref, leaf_table, parent_table, top_table,
               m2l_hbm, l2l_ref, packed_ref, near_ref, wave_ref, mix_ref, factor_ref, out_ref,
               gathered, pool, acc, m2l, local, leaf_local, spread, done, sem):
    leaves = counts_ref.shape[0]
    mid, top = leaves // 8, leaves // 64
    rows = places_ref.shape[0]
    slots = places_ref.shape[1]
    tiles = local.shape[0]
    first = base_ref[0]
    fetch = pltpu.make_async_copy(m2l_hbm, m2l, sem)
    fetch.start()
    wide = lax.broadcasted_iota(jnp.int32, (8, pool.shape[0]), 1)

    def gather_from(table):
        def body(group, carry):
            for slot in range(NEIGHBOURS + 1):
                pool[8 * slot:8 * slot + 8, :] = table[blocks_ref[group, slot]].astype(F32)
            start = pl.multiple_of(group * 8, 8)
            places = places_ref[pl.ds(start, 8), :]
            hits = [jnp.where(places[:, t:t + 1] == wide, 1.0, 0.0) for t in range(slots)]
            picked = dot(jnp.concatenate(hits, axis=0).astype(BF16), pool[...].astype(BF16))
            for t in range(slots):
                gathered[t, pl.ds(start, 8), :] = picked[8 * t:8 * t + 8, :]
            return carry

        return body

    lax.fori_loop(0, mid, gather_from(leaf_table), 0)
    lax.fori_loop(mid, mid + top, gather_from(parent_table), 0)
    lax.fori_loop(mid + top, rows // 8, gather_from(top_table), 0)

    fetch.wait()
    acc[...] = jnp.zeros_like(acc)
    step = 4

    def translate(part, carry):
        total = jnp.zeros((rows, coeffs), F32)
        for inner in range(step):
            t = part * step + inner
            total = total + dot(gathered[t].astype(BF16), m2l[t])
        acc[...] += total
        return carry

    lax.fori_loop(0, slots // step, translate, 0)

    def spread_down(value, count):
        for which in range(8):
            child = dot(value, l2l_ref[which])
            for tile in range(tiles):
                low_col = tile * LANES
                width = min(LANES, coeffs - low_col)
                part = child[:count, low_col:low_col + width]
                if width < LANES:
                    part = jnp.concatenate([part, jnp.zeros((count, LANES - width), F32)], axis=1)
                local[tile, pl.ds(which, count, stride=8), :] = part
        return jnp.concatenate([local[tile, 0:8 * count, :] for tile in range(tiles)], axis=1)

    grand = acc[leaves + mid:, :] * 0.25
    middle = spread_down(grand.astype(BF16), top)[:, :coeffs] + acc[leaves:leaves + mid, :] * 0.5
    down = spread_down(middle.astype(BF16), mid)
    leaf_local[...] = down
    leaf_local[:, :coeffs] = down[:, :coeffs] + acc[0:leaves, :]
    flipped = jnp.transpose(leaf_local[...])[:coeffs, :]
    high, low = kernel_split2(flipped)
    spread[0:coeffs, :] = high
    spread[coeffs:, :] = low

    total = jnp.int32(0)

    def count_up(leaf, offset):
        return offset + counts_ref[leaf]

    total = lax.fori_loop(0, leaves, count_up, jnp.int32(0))

    def evaluate(block, carry):
        value = packed_ref[block]
        features, ids = block_features(value)
        wave_part = dot(wave_ref[...], feature_pieces(features))
        local_id = jnp.broadcast_to(ids - first, (leaves, LANES))
        hits = lax.broadcasted_iota(jnp.int32, (leaves, LANES), 0) == local_id
        both = dot(spread[...], jnp.where(hits, 1.0, 0.0).astype(BF16))
        product = cos_turns(wave_part) * (both[:coeffs] + both[coeffs:])
        high, low = kernel_split2(product)
        mixed = dot(mix_ref[...], high)
        mixed_low = dot(mix_ref[...], low)
        far = mixed[0:8] + (mixed[8:16] + mixed_low[0:8])
        drop = jnp.broadcast_to(value[6:7, :].astype(jnp.int32), (factor_ref.shape[1], LANES))
        pick = lax.broadcasted_iota(jnp.int32, drop.shape, 0) == drop
        parts = dot(factor_ref[...], jnp.where(pick, 1.0, 0.0).astype(BF16))
        factor = parts[0:1] + (parts[1:2] + parts[2:3])
        done[block] = (near_ref[block] + far) * factor
        return carry

    lax.fori_loop(0, (total + LANES - 1) >> 7, evaluate, 0)

    lane = lax.broadcasted_iota(jnp.int32, (8, LANES), 1)

    def unpack(pair, offset):
        result = jnp.zeros((8, LANES), F32)
        for half in range(2):
            count = counts_ref[2 * pair + half]
            block, place = offset >> 7, offset & 127
            merged = jnp.where(lane >= place, done[block], done[block + 1])
            turned = pltpu.roll(merged, (64 * half - place) & 127, 1)
            result = jnp.where((lane >= 64 * half) & (lane < 64 * half + count), turned, result)
            offset = offset + count
        out_ref[:, pl.ds(pl.multiple_of(pair * LANES, LANES), LANES)] = result[0:3, :]
        return offset

    lax.fori_loop(0, leaves // 2, unpack, jnp.int32(0))


def far_field(first_leaf, counts, blocks, places, tables, m2l, l2l, packed, near, wave, mix, factor):
    leaves, coeffs = counts.shape[0], m2l.shape[1]
    tiles = -(-coeffs // LANES)
    rows = places.shape[0]
    smem = pl.BlockSpec(memory_space=pltpu.SMEM)
    vmem = pl.BlockSpec(memory_space=pltpu.VMEM)
    anywhere = pl.BlockSpec(memory_space=pl.ANY)
    return pl.pallas_call(
        functools.partial(far_kernel, coeffs),
        out_shape=jax.ShapeDtypeStruct((3, leaves * PTS), F32),
        in_specs=[smem, smem, smem] + [vmem] * 4 + [anywhere] + [vmem] * 6,
        out_specs=vmem,
        scratch_shapes=[
            pltpu.VMEM((m2l.shape[0], rows, coeffs), F32),
            pltpu.VMEM(((NEIGHBOURS + 1) * 8, coeffs), F32),
            pltpu.VMEM((rows, coeffs), F32),
            pltpu.VMEM(m2l.shape, BF16),
            pltpu.VMEM((tiles, leaves, LANES), F32),
            pltpu.VMEM((leaves, tiles * LANES), F32),
            pltpu.VMEM((2 * coeffs, leaves), BF16),
            pltpu.VMEM(packed.shape, F32),
            pltpu.SemaphoreType.DMA,
        ],
        compiler_params=params(60),
        name="far_field",
    )(first_leaf, counts, blocks, places, *tables, m2l, l2l, packed, near, wave, mix, factor)


def shards(points, forces, counts, droplet, contrast, ulist, vlist0, vlist1, vlist2,
           wave, phases, p2m_mix, m2m, m2l, l2l, l2p_mix):
    both = ("grp", "sub")
    leaves = counts.shape[0]
    coeffs = m2l.shape[1]
    group_leaves = leaves * lax.axis_size("sub")
    all_leaves = group_leaves * lax.axis_size("grp")
    device = lax.axis_index(both)
    first = device * leaves
    first_arg = first.astype(jnp.int32).reshape(1)

    ids = (first + jnp.arange(leaves * PTS, dtype=jnp.int32) // PTS).astype(F32)[None, :]
    slots = jnp.concatenate([points, forces, droplet.astype(F32)[None, :], ids], axis=0)

    width = HALO * PTS
    count_row = jnp.repeat(counts, PTS).astype(F32)[None, :]
    edge = lambda part: jnp.concatenate(
        [slots[0:6, part], count_row[:, part], slots[7:8, part]], axis=0
    )
    devices = lax.axis_size(both)
    right_way = [(i, i + 1) for i in range(devices - 1)]
    left_way = [(i + 1, i) for i in range(devices - 1)]
    left = lax.ppermute(edge(slice(leaves * PTS - width, None)), both, right_way)
    right = lax.ppermute(edge(slice(0, width)), both, left_way)
    left_counts = left[6].reshape(HALO, PTS)[:, 0].astype(jnp.int32)
    right_counts = right[6].reshape(HALO, PTS)[:, 0].astype(jnp.int32)

    turns = 1.0 / (2.0 * math.pi)
    up_weights = jnp.concatenate(
        [weight_rows(wave * turns, 0, phases[0] * turns), weight_rows(p2m_mix, 3)], axis=0
    )
    packed, leaf_mult, up = upward_pass(first_arg, counts, slots, up_weights, m2m)

    mid, top = leaves // 8, leaves // 64
    group = lax.all_gather(leaf_mult, "sub", axis=0, tiled=True)
    above = lax.all_gather(up[:mid + top], both, axis=0, tiled=True).reshape(devices, mid + top, coeffs)
    tables = (
        group.reshape(-1, 8, coeffs),
        above[:, :mid].reshape(-1, 8, coeffs),
        above[:, mid:].reshape(-1, 8, coeffs),
    )

    local_list = jnp.where(ulist >= 0, ulist - first + HALO, -1)
    near = near_field(first_arg, counts, left_counts, right_counts, packed, left, right, local_list)

    rows0 = first + jnp.arange(leaves, dtype=jnp.int32)
    rows1 = device * mid + jnp.arange(mid, dtype=jnp.int32)
    rows2 = device * top + jnp.arange(top, dtype=jnp.int32)
    places = jnp.concatenate(
        [
            list_places(vlist0, rows0 >> 3, ROOT_BITS - 1),
            list_places(vlist1, rows1 >> 3, ROOT_BITS - 2),
            jnp.pad(list_places(vlist2, rows2 >> 3, ROOT_BITS - 3), ((0, 8 - top), (0, 0)), constant_values=-1),
        ],
        axis=0,
    )
    group_parents = group_leaves // 8
    parents0 = rows0[::8] >> 3
    blocks = jnp.concatenate(
        [
            pool_blocks(parents0, ROOT_BITS - 1, lax.axis_index("grp") * group_parents, group_parents),
            pool_blocks(rows1[::8] >> 3, ROOT_BITS - 2, 0, all_leaves // 64),
            pool_blocks(rows2[:1] >> 3, ROOT_BITS - 3, 0, all_leaves // 512),
        ],
        axis=0,
    )
    down_weights = weight_rows(wave * turns, 0, phases[1] * turns)
    mix_high, mix_low, _ = split3(l2p_mix)
    mix = jnp.concatenate(
        [jnp.pad(mix_high, ((0, 5), (0, 0))), jnp.pad(mix_low, ((0, 5), (0, 0)))], axis=0
    ).astype(BF16)
    factor = jnp.pad(jnp.stack(split3(2.0 / (1.0 + contrast))), ((0, 13), (0, 0))).astype(BF16)
    return far_field(first_arg, counts, blocks, places, tables, m2l, l2l, packed, near,
                     down_weights, mix, factor)


def solution(mesh):
    spread = P(("grp", "sub"))
    rows = P(("grp", "sub"), None)
    columns = P(None, ("grp", "sub"))
    return jax.shard_map(
        shards,
        mesh=mesh,
        in_specs=(
            columns, columns, spread, spread, P(), rows, rows, rows, rows,
            P(), P(), P(), P(), P(), P(), P(),
        ),
        out_specs=columns,
        check_vma=False,
    )
```

```python
import functools
import math

import jax
import jax.numpy as jnp
from jax import lax
from jax.experimental import pallas as pl
from jax.experimental.pallas import tpu as pltpu
from jax.sharding import PartitionSpec as P

PTS = 64
HALO = 16
EPS_SQ = 0.3 * 0.3
LANES = 128
NEIGHBOURS = 27
ROOT_BITS = 5

F32 = jnp.float32
BF16 = jnp.bfloat16

COS_COEFFS = (
    0.9999999890590235,
    -19.739204499453994,
    64.93911745989843,
    -85.45013953092186,
    60.167630951185615,
    -25.967599249120923,
    6.528658161956132,
)

NT = (((1,), (1,)), ((), ()))
NN = (((1,), (0,)), ((), ()))


def params(megabytes):
    return pltpu.CompilerParams(vmem_limit_bytes=megabytes * 1024 * 1024)


def dot(left, right, dims=NN):
    return lax.dot_general(left, right, dims, preferred_element_type=F32)


def kernel_split3(value):
    high = value.astype(BF16).astype(F32)
    rest = value - high
    middle = rest.astype(BF16).astype(F32)
    return high, middle, rest - middle


def kernel_split2(value):
    high = value.astype(BF16)
    return high, (value - high.astype(F32)).astype(BF16)


def stack_rows(pieces, rows):
    shape = (rows, pieces[0].shape[1])
    row = lax.broadcasted_iota(jnp.int32, shape, 0)
    result = jnp.zeros(shape, F32)
    for k, piece in enumerate(pieces):
        result = jnp.where(row == k, jnp.broadcast_to(piece, shape), result)
    return result


def weight_pieces(matrix, bias):
    high, middle, low = kernel_split3(matrix)
    shift = stack_rows(kernel_split3(bias), 8)
    pieces = [high, high, middle, middle, high, low, shift]
    pieces.append(jnp.zeros((LANES - 56, matrix.shape[1]), F32))
    return jnp.transpose(jnp.concatenate(pieces, axis=0))[:, :64].astype(BF16)


def feature_pieces(rows):
    high, middle, low = kernel_split3(rows)
    ones = jnp.where(lax.broadcasted_iota(jnp.int32, rows.shape, 0) < 3, 1.0, 0.0)
    pieces = [high, middle, high, middle, low, high, ones, jnp.zeros_like(rows)]
    return jnp.concatenate(pieces, axis=0).astype(BF16)


def cos_turns(turns):
    part = turns - jnp.round(turns)
    square = part * part
    value = jnp.full_like(square, COS_COEFFS[-1])
    for coeff in COS_COEFFS[-2::-1]:
        value = value * square + coeff
    return value


def center_rows(ids):
    axis = lax.broadcasted_iota(jnp.int32, ids.shape, 0)
    total = jnp.zeros_like(ids)
    for bit in range(ROOT_BITS):
        total = total + (((ids >> (axis + 3 * bit)) & 1) << bit)
    return total.astype(F32) + 0.5


def block_features(block):
    row = lax.broadcasted_iota(jnp.int32, block.shape, 0)
    ids = block[7:8, :].astype(jnp.int32)
    centers = center_rows(jnp.broadcast_to(jnp.maximum(ids, 0), block.shape))
    rows = jnp.where(row < 3, block - centers, jnp.where(row < 6, block, 0.0))
    return rows, ids


def wide_features(packed_ref, block, first):
    pieces, leaves = [], []
    for step in range(2):
        rows, ids = block_features(packed_ref[block + step])
        pieces.append(feature_pieces(rows))
        leaves.append(ids - first)
    return jnp.concatenate(pieces, axis=1), jnp.concatenate(leaves, axis=1)


def pack_leaves(read_pair, count_of, pairs, dest, start, current):
    lane = lax.broadcasted_iota(jnp.int32, (8, LANES), 1)

    def body(part, carry):
        offset, held = carry
        for inner in range(8):
            pair = part * 8 + inner
            value = read_pair(pair)
            for half in range(2):
                count = count_of(2 * pair + half)
                block, place = offset >> 7, offset & 127
                rolled = pltpu.roll(value, (place + 64 * half) & 127, 1)
                merged = jnp.where(lane >= place, rolled, held)
                dest[block] = merged
                held = jnp.where(place + count >= LANES, rolled, merged)
                offset = offset + count
        return offset, held

    offset, held = lax.fori_loop(0, pairs // 8, body, (start, current))
    dest[offset >> 7] = held
    return offset


def finish_pack(dest, end, more):
    lane = lax.broadcasted_iota(jnp.int32, (8, LANES), 1)
    row = lax.broadcasted_iota(jnp.int32, (8, LANES), 0)
    block, place = end >> 7, end & 127
    empty = jnp.where(row == 7, -1.0, 0.0)
    dest[block] = jnp.where(lane >= place, empty, dest[block])
    for step in range(more):
        dest[block + 1 + step] = empty


def space_order(parent):
    x0, y0, z0, x1, y1 = ((parent >> bit) & 1 for bit in range(5))
    return (z0 * 4 + y1 * 2 + y0) * 4 + x1 * 2 + x0


def upward_kernel(coeffs, base_ref, counts_ref, slots_ref, constants_ref, m2m_ref,
                  packed_ref, leaf_ref, up_ref, acc, staged, parents, weights):
    leaves = counts_ref.shape[0]
    lane = lax.broadcasted_iota(jnp.int32, (8, LANES), 1)

    def read_pair(pair):
        return slots_ref[:, pl.ds(pl.multiple_of(pair * LANES, LANES), LANES)]

    total = pack_leaves(
        read_pair, lambda leaf: counts_ref[leaf], leaves // 2, packed_ref,
        jnp.int32(0), jnp.zeros((8, LANES), F32),
    )
    finish_pack(packed_ref, total, 3)
    weights[...] = weight_pieces(constants_ref[0:8, :], constants_ref[8:9, :])
    acc[...] = jnp.zeros_like(acc)
    first = base_ref[0]

    def body(part, carry):
        left_side, right_side = [], []
        for inner in range(2):
            features, local = wide_features(packed_ref, part * 4 + inner * 2, first)
            both = dot(weights[0:2 * coeffs, :], features)
            high, low = kernel_split2(cos_turns(both[:coeffs]) * both[coeffs:])
            hits = lax.broadcasted_iota(jnp.int32, (leaves, 2 * LANES), 0) == local
            which = jnp.where(hits, 1.0, 0.0).astype(BF16)
            left_side += [which, which]
            right_side += [high, low]
        acc[...] += dot(jnp.concatenate(left_side, axis=1), jnp.concatenate(right_side, axis=1), NT)
        return carry

    lax.fori_loop(0, (total + 4 * LANES - 1) >> 9, body, 0)
    leaf = acc[...].astype(BF16)
    leaf_f32 = leaf.astype(F32)
    for parent in range(leaves // 8):
        place = 8 * space_order(parent)
        acc[place:place + 8, :] = leaf_f32[8 * parent:8 * parent + 8, :]
    leaf_ref[...] = acc[...].astype(BF16)
    tiles = staged.shape[0]

    def stage(target, value):
        for tile in range(tiles):
            low_col = tile * LANES
            width = min(LANES, coeffs - low_col)
            target[tile, :, :width] = value[:, low_col:low_col + width]

    def child(source, which, rows):
        parts = [source[tile, pl.ds(which, rows, stride=8), :] for tile in range(tiles)]
        return jnp.concatenate(parts, axis=1)[:, :coeffs].astype(BF16)

    stage(staged, leaf_f32)
    above = jnp.zeros((leaves // 8, coeffs), F32)
    for which in range(8):
        above = above + dot(child(staged, which, leaves // 8), m2m_ref[which])
    up = above.astype(BF16)
    stage(parents, up.astype(F32))
    top = jnp.zeros((leaves // 64, coeffs), F32)
    for which in range(8):
        top = top + dot(child(parents, which, leaves // 64), m2m_ref[which])
    half = jnp.zeros_like(top)
    odd = ((first // leaves) & 1) == 1
    block = jnp.concatenate([jnp.where(odd, half, top), jnp.where(odd, top, half)], axis=0)
    up_ref[...] = jnp.concatenate([above, block], axis=0).astype(BF16)


def upward_pass(first_leaf, counts, slots, constants, m2m):
    leaves, coeffs = counts.shape[0], m2m.shape[1]
    blocks = slots.shape[1] // LANES
    tiles = -(-coeffs // LANES)
    smem = pl.BlockSpec(memory_space=pltpu.SMEM)
    vmem = pl.BlockSpec(memory_space=pltpu.VMEM)
    up_rows = leaves // 8 + 8
    return pl.pallas_call(
        functools.partial(upward_kernel, coeffs),
        out_shape=(
            jax.ShapeDtypeStruct((blocks + 4, 8, LANES), F32),
            jax.ShapeDtypeStruct((leaves, coeffs), BF16),
            jax.ShapeDtypeStruct((up_rows, coeffs), BF16),
        ),
        in_specs=[smem, smem] + [vmem] * 3,
        out_specs=(vmem, vmem, vmem),
        scratch_shapes=[
            pltpu.VMEM((leaves, coeffs), F32),
            pltpu.VMEM((tiles, leaves, LANES), F32),
            pltpu.VMEM((tiles, leaves // 8, LANES), F32),
            pltpu.VMEM((constants.shape[1], 64), BF16),
        ],
        compiler_params=params(32),
        name="upward",
    )(first_leaf, counts, slots, constants, m2m)


def near_kernel(base_ref, counts_ref, left_counts, right_counts, packed_ref, left_ref, right_ref,
                ulist_ref, near_ref, sources, which_source, lists, shares, columns,
                targets, share_a, share_b, acc, starts, lows, highs):
    leaves = counts_ref.shape[0]
    window = leaves + 2 * HALO
    halo_blocks = HALO * PTS // LANES
    first = base_ref[0]
    lane = lax.broadcasted_iota(jnp.int32, (8, LANES), 1)
    row = lax.broadcasted_iota(jnp.int32, (8, LANES), 0)
    empty = jnp.where(row == 7, -1.0, 0.0)

    left_total = jnp.int32(0)
    for leaf in range(HALO):
        left_total = left_total + left_counts[leaf]
    left_start = HALO * PTS - left_total

    def note_left(leaf, offset):
        starts[leaf] = offset
        return offset + left_counts[leaf]

    offset = lax.fori_loop(0, HALO, note_left, left_start)

    def note_own(leaf, offset):
        starts[HALO + leaf] = offset
        return offset + counts_ref[leaf]

    own_end = lax.fori_loop(0, leaves, note_own, offset)

    def note_right(leaf, offset):
        starts[HALO + leaves + leaf] = offset
        return offset + right_counts[leaf]

    end = lax.fori_loop(0, HALO, note_right, own_end)
    starts[window] = end

    def pair_of(ref):
        return lambda pair: ref[:, pl.ds(pl.multiple_of(pair * LANES, LANES), LANES)]

    pack_leaves(pair_of(left_ref), lambda leaf: left_counts[leaf], HALO // 2, sources, left_start, empty)
    own_blocks = (own_end - HALO * PTS + LANES - 1) >> 7

    def copy_block(block, carry):
        sources[halo_blocks + block] = packed_ref[block]
        return carry

    lax.fori_loop(0, own_blocks, copy_block, 0)
    held = sources[own_end >> 7]
    pack_leaves(pair_of(right_ref), lambda leaf: right_counts[leaf], HALO // 2, sources, own_end, held)
    finish_pack(sources, end, 3)

    own_list = ulist_ref[...]
    column = lax.broadcasted_iota(jnp.int32, (leaves, window), 1)
    times = jnp.zeros((leaves, window), F32)
    for slot in range(own_list.shape[1]):
        times = times + jnp.where(own_list[:, slot:slot + 1] == column, 1.0, 0.0)
    lists[...] = times.astype(BF16)

    def mark_source(tile, carry):
        ids = sources[tile][7:8, :].astype(jnp.int32)
        local = jnp.broadcast_to(jnp.where(ids < 0, -1, ids - first + HALO), (window, LANES))
        hits = lax.broadcasted_iota(jnp.int32, (window, LANES), 0) == local
        which_source[tile] = jnp.where(hits, 1.0, 0.0).astype(BF16)
        return carry

    lax.fori_loop(left_start >> 7, (end >> 7) + 4, mark_source, 0)

    def mark_targets(part, carry):
        for inner in range(4):
            block = part * 4 + inner
            padded = jnp.concatenate([packed_ref[block], jnp.zeros((LANES - 8, LANES), F32)], axis=0)
            turned = jnp.transpose(padded)
            columns[block] = turned
            ids = turned[:, 7:8].astype(jnp.int32) - first
            hits = lax.broadcasted_iota(jnp.int32, (LANES, leaves), 1) == ids
            shares[block] = dot(jnp.where(hits, 1.0, 0.0).astype(BF16), lists[...]).astype(BF16)
            live = padded[7:8, :]
            low_leaf = jnp.min(jnp.where(live < 0.0, 1e9, live)).astype(jnp.int32) - first
            high_leaf = jnp.max(live).astype(jnp.int32) - first
            lows[block] = starts[jnp.clip(low_leaf, 0, leaves - 1)] >> 7
            highs[block] = (starts[jnp.clip(high_leaf, 0, leaves - 1) + 2 * HALO + 1] + LANES - 1) >> 7
        return carry

    lax.fori_loop(0, (own_blocks + 3) >> 2, mark_targets, 0)
    ones = jnp.ones((8, 2 * LANES), BF16)

    def close_block(block):
        rows = []
        for axis in range(3):
            high, low = kernel_split2(acc[block & 1, axis])
            rows.append(dot(ones, jnp.concatenate([high, low], axis=1), NT)[0:1, :])
        near_ref[block] = stack_rows(rows, 8) * (1.0 / (8.0 * math.pi))

    def target_block(block, carry):
        close_block(jnp.maximum(block - 1, 0))
        now = block & 1
        acc[now] = jnp.zeros(acc.shape[1:], F32)
        turned = columns[block]
        for axis in range(3):
            targets[axis] = jnp.broadcast_to(turned[:, axis:axis + 1], (LANES, LANES))
        source_low, source_high = lows[block], highs[block]
        share_a[...] = dot(shares[block], which_source[source_low])

        def source_tile(tile, share):
            value = sources[tile]
            feature = [jnp.broadcast_to(value[k:k + 1, :], (8, LANES)) for k in range(6)]
            for chunk in range(LANES // 8):
                span = slice(8 * chunk, 8 * chunk + 8)
                dx = targets[0, span, :] - feature[0]
                dy = targets[1, span, :] - feature[1]
                dz = targets[2, span, :] - feature[2]
                dist_sq = dx * dx + dy * dy + (dz * dz + EPS_SQ)
                along = dx * feature[3] + dy * feature[4] + dz * feature[5]
                inverse = lax.rsqrt(dist_sq)
                weighted = share[span, :] * inverse
                cubed = weighted * (inverse * inverse)
                plain = weighted + EPS_SQ * cubed
                outer = along * cubed
                acc[now, 0, span, :] += plain * feature[3] + outer * dx
                acc[now, 1, span, :] += plain * feature[4] + outer * dy
                acc[now, 2, span, :] += plain * feature[5] + outer * dz

        def two_tiles(part, carry):
            tile = source_low + 2 * part
            share_b[...] = dot(shares[block], which_source[tile + 1])
            source_tile(tile, share_a)
            share_a[...] = dot(shares[block], which_source[tile + 2])
            source_tile(tile + 1, share_b)
            return carry

        lax.fori_loop(0, (source_high - source_low) >> 1, two_tiles, 0)

        @pl.when(((source_high - source_low) & 1) == 1)
        def _():
            source_tile(source_high - 1, share_a)

        return carry

    lax.fori_loop(0, own_blocks, target_block, 0)
    close_block(own_blocks - 1)


def near_field(first_leaf, counts, left_counts, right_counts, packed, left, right, ulist):
    leaves = counts.shape[0]
    window = leaves + 2 * HALO
    blocks = packed.shape[0]
    source_blocks = (leaves + 2 * HALO) * PTS // LANES + 4
    smem = pl.BlockSpec(memory_space=pltpu.SMEM)
    vmem = pl.BlockSpec(memory_space=pltpu.VMEM)
    return pl.pallas_call(
        near_kernel,
        out_shape=jax.ShapeDtypeStruct((blocks, 8, LANES), F32),
        in_specs=[smem] * 4 + [vmem] * 4,
        out_specs=vmem,
        scratch_shapes=[
            pltpu.VMEM((source_blocks, 8, LANES), F32),
            pltpu.VMEM((source_blocks, window, LANES), BF16),
            pltpu.VMEM((leaves, window), BF16),
            pltpu.VMEM((blocks + 2, LANES, window), BF16),
            pltpu.VMEM((blocks + 2, LANES, LANES), F32),
            pltpu.VMEM((3, LANES, LANES), F32),
            pltpu.VMEM((LANES, LANES), F32),
            pltpu.VMEM((LANES, LANES), F32),
            pltpu.VMEM((2, 3, LANES, LANES), F32),
            pltpu.SMEM((window + 1,), jnp.int32),
            pltpu.SMEM((blocks,), jnp.int32),
            pltpu.SMEM((blocks,), jnp.int32),
        ],
        compiler_params=params(56),
        cost_estimate=pl.CostEstimate(flops=20_000_000_000, bytes_accessed=2_000_000, transcendentals=0),
        name="near_field",
    )(first_leaf, counts, left_counts, right_counts, packed, left, right, ulist)


def coords_of(code, bits):
    return [
        sum(((code >> (3 * bit + axis)) & 1) << bit for bit in range(bits)) for axis in range(3)
    ]


def code_of(coords, bits):
    return sum(
        ((coords[axis] >> bit) & 1) << (3 * bit + axis) for axis in range(3) for bit in range(bits)
    )


def list_places(vlist, parent_of_row, bits):
    own = coords_of(parent_of_row[:, None], bits)
    other = coords_of(vlist >> 3, bits)
    near = sum((o - m + 1) * 3 ** axis for axis, (o, m) in enumerate(zip(other, own)))
    slot = jnp.where(jnp.arange(vlist.shape[1])[None, :] == 0, NEIGHBOURS, near)
    return jnp.where(vlist >= 0, slot * 8 + (vlist & 7), -1)


def pool_steps():
    slot = jnp.arange(NEIGHBOURS + 1, dtype=jnp.int32)[None, :]
    return (slot % 3 - 1, slot // 3 % 3 - 1, slot // 9 % 3 - 1), slot == NEIGHBOURS


def upper_blocks(parents, bits, extent):
    steps, mirror = pool_steps()
    own = coords_of(parents[:, None], bits)
    code = code_of([jnp.clip(m + s, 0, 2 ** bits - 1) for m, s in zip(own, steps)], bits)
    return jnp.where(mirror, (parents[:, None] + extent // 2) % extent, code)


def leaf_blocks():
    steps, mirror = pool_steps()
    parent = jnp.arange(32, dtype=jnp.int32)[:, None]
    x = (parent & 1) + ((parent >> 3) & 1) * 2
    y = ((parent >> 1) & 1) + ((parent >> 4) & 1) * 2
    z = (parent >> 2) & 1
    at = (z * 4 + y) * 4 + x
    x, y, z = x + steps[0], y + steps[1], z + steps[2]
    x_out, y_out, z_out = (x < 0) | (x > 3), (y < 0) | (y > 3), (z < 0) | (z > 1)
    x, y = jnp.where(x_out, 4, x), jnp.where(y_out, 4, y)
    inside = jnp.where(
        y_out, 40 + z * 5 + x, jnp.where(x_out, 32 + z * 4 + y, (z * 4 + y) * 4 + x)
    )
    outside = jnp.where(z < 0, 50, 75) + y * 5 + x
    return jnp.where(mirror, 100 + at, jnp.where(z_out, outside, inside))


def far_kernel(coeffs, base_ref, counts_ref, blocks_ref, places_ref, *rest):
    (own_ref, x_ref, y_ref, below_ref, above_ref, mirror_ref, upper_table,
     m2l_hbm, l2l_ref, packed_ref, near_ref, constants_ref, contrast_ref, out_ref,
     gathered, table, pool, acc, m2l, local, leaf_local, spread, done, weights, sem) = rest
    leaves = counts_ref.shape[0]
    mid, top = leaves // 8, leaves // 64
    rows = places_ref.shape[0]
    slots = places_ref.shape[1]
    tiles = local.shape[0]
    first = base_ref[0]
    fetch = pltpu.make_async_copy(m2l_hbm, m2l, sem)
    fetch.start()
    weights[...] = weight_pieces(constants_ref[0:8, :], constants_ref[9:10, :])
    wide = lax.broadcasted_iota(jnp.int32, (8, pool.shape[1]), 1)

    filled = 0
    for piece in (own_ref, x_ref, y_ref, below_ref, above_ref, mirror_ref):
        table[filled:filled + piece.shape[0]] = piece[...].astype(F32)
        filled += piece.shape[0]

    def gather_from(source, width, halves):
        def body(part, carry):
            for inner in range(width):
                group = part * width + inner
                for slot in range(NEIGHBOURS + 1):
                    at = blocks_ref[group, slot]
                    value = source[at].astype(F32)
                    if halves:
                        value = value + source[at + 5].astype(F32)
                    pool[inner, 8 * slot:8 * slot + 8, :] = value
                start = pl.multiple_of(group * 8, 8)
                places = places_ref[pl.ds(start, 8), :]
                hits = [jnp.where(places[:, t:t + 1] == wide, 1.0, 0.0) for t in range(slots)]
                picked = dot(jnp.concatenate(hits, axis=0).astype(BF16), pool[inner].astype(BF16))
                for t in range(slots):
                    gathered[t, pl.ds(start, 8), :] = picked[8 * t:8 * t + 8, :]
            return carry

        return body

    lax.fori_loop(0, mid // 4, gather_from(table, 4, False), 0)
    lax.fori_loop(mid // 4, (mid + top) // 4, gather_from(upper_table, 4, False), 0)
    lax.fori_loop(mid + top, rows // 8, gather_from(upper_table, 1, True), 0)

    fetch.wait()
    acc[...] = jnp.zeros_like(acc)
    step = 4

    def translate(part, carry):
        total = jnp.zeros((rows, coeffs), F32)
        for inner in range(step):
            t = part * step + inner
            total = total + dot(gathered[t].astype(BF16), m2l[t])
        acc[...] += total
        return carry

    lax.fori_loop(0, slots // step, translate, 0)

    def spread_down(value, count):
        for which in range(8):
            child = dot(value, l2l_ref[which])
            for tile in range(tiles):
                low_col = tile * LANES
                width = min(LANES, coeffs - low_col)
                part = child[:count, low_col:low_col + width]
                if width < LANES:
                    part = jnp.concatenate([part, jnp.zeros((count, LANES - width), F32)], axis=1)
                local[tile, pl.ds(which, count, stride=8), :] = part
        return jnp.concatenate([local[tile, 0:8 * count, :] for tile in range(tiles)], axis=1)

    grand = acc[leaves + mid:, :] * 0.25
    middle = spread_down(grand.astype(BF16), top)[:, :coeffs] + acc[leaves:leaves + mid, :] * 0.5
    down = spread_down(middle.astype(BF16), mid)
    leaf_local[...] = down
    leaf_local[:, :coeffs] = down[:, :coeffs] + acc[0:leaves, :]
    flipped = jnp.transpose(leaf_local[...])[:coeffs, :]
    high, low = kernel_split2(flipped)
    spread[0:coeffs, :] = high
    spread[coeffs:, :] = low

    total = jnp.int32(0)

    def count_up(leaf, offset):
        return offset + counts_ref[leaf]

    total = lax.fori_loop(0, leaves, count_up, jnp.int32(0))

    mix_high, mix_low, _ = kernel_split3(constants_ref[16:24, 0:coeffs])
    mix = jnp.concatenate([mix_high, mix_low], axis=0).astype(BF16)
    factors = stack_rows(kernel_split3(2.0 / (1.0 + contrast_ref[0:1, :])), 16).astype(BF16)

    def evaluate(part, carry):
        for inner in range(2):
            block = part * 4 + inner * 2
            features, local_id = wide_features(packed_ref, block, first)
            turns = dot(weights[0:coeffs, :], features)
            hits = lax.broadcasted_iota(jnp.int32, (leaves, 2 * LANES), 0) == local_id
            both = dot(spread[...], jnp.where(hits, 1.0, 0.0).astype(BF16))
            product = cos_turns(turns) * (both[:coeffs] + both[coeffs:])
            high, low = kernel_split2(product)
            mixed, mixed_low = dot(mix, high), dot(mix, low)
            far = mixed[0:8] + (mixed[8:16] + mixed_low[0:8])
            drop = jnp.concatenate([packed_ref[block + step][6:7, :] for step in range(2)], axis=1)
            pick = lax.broadcasted_iota(jnp.int32, (factors.shape[1], 2 * LANES), 0) == drop.astype(jnp.int32)
            parts = dot(factors, jnp.where(pick, 1.0, 0.0).astype(BF16))
            factor = parts[0:1] + (parts[1:2] + parts[2:3])
            for step in range(2):
                span = slice(step * LANES, (step + 1) * LANES)
                done[block + step] = (near_ref[block + step] + far[:, span]) * factor[:, span]
        return carry

    lax.fori_loop(0, (total + 4 * LANES - 1) >> 9, evaluate, 0)

    lane = lax.broadcasted_iota(jnp.int32, (8, LANES), 1)

    def unpack(part, offset):
        for inner in range(8):
            pair = part * 8 + inner
            result = jnp.zeros((8, LANES), F32)
            for half in range(2):
                count = counts_ref[2 * pair + half]
                block, place = offset >> 7, offset & 127
                merged = jnp.where(lane >= place, done[block], done[block + 1])
                turned = pltpu.roll(merged, (64 * half - place) & 127, 1)
                result = jnp.where((lane >= 64 * half) & (lane < 64 * half + count), turned, result)
                offset = offset + count
            out_ref[:, pl.ds(pl.multiple_of(pair * LANES, LANES), LANES)] = result[0:3, :]
        return offset

    lax.fori_loop(0, leaves // 16, unpack, jnp.int32(0))


def far_field(first_leaf, counts, blocks, places, pieces, upper, m2l, l2l, packed, near,
              constants, contrast):
    leaves, coeffs = counts.shape[0], m2l.shape[1]
    tiles = -(-coeffs // LANES)
    rows = places.shape[0]
    table_blocks = sum(piece.shape[0] for piece in pieces)
    smem = pl.BlockSpec(memory_space=pltpu.SMEM)
    vmem = pl.BlockSpec(memory_space=pltpu.VMEM)
    anywhere = pl.BlockSpec(memory_space=pl.ANY)
    return pl.pallas_call(
        functools.partial(far_kernel, coeffs),
        out_shape=jax.ShapeDtypeStruct((3, leaves * PTS), F32),
        in_specs=[smem] * 3 + [vmem] * 8 + [anywhere] + [vmem] * 5,
        out_specs=vmem,
        scratch_shapes=[
            pltpu.VMEM((m2l.shape[0], rows, coeffs), F32),
            pltpu.VMEM((table_blocks, 8, coeffs), F32),
            pltpu.VMEM((4, (NEIGHBOURS + 1) * 8, coeffs), F32),
            pltpu.VMEM((rows, coeffs), F32),
            pltpu.VMEM(m2l.shape, BF16),
            pltpu.VMEM((tiles, leaves, LANES), F32),
            pltpu.VMEM((leaves, tiles * LANES), F32),
            pltpu.VMEM((2 * coeffs, leaves), BF16),
            pltpu.VMEM(packed.shape, F32),
            pltpu.VMEM((constants.shape[1], 64), BF16),
            pltpu.SemaphoreType.DMA,
        ],
        compiler_params=params(60),
        name="far_field",
    )(first_leaf, counts, blocks, places, *pieces, upper, m2l, l2l, packed, near, constants, contrast)


def leaf_pieces(own, sub):
    coeffs = own.shape[2]
    box = own.reshape(2, 4, 4, 8, coeffs)
    x_side, y_side = (sub >> 1) & 1, (sub >> 2) & 1
    swap = lambda value, bit: lax.ppermute(value, "sub", [(i, i ^ bit) for i in range(16)])
    mirror = swap(own, 8)
    x_face = swap(lax.dynamic_index_in_dim(box, 3 - 3 * x_side, 2, keepdims=False), 2)
    wider = jnp.concatenate([box, x_face[:, :, None]], axis=2)
    y_face = swap(lax.dynamic_index_in_dim(wider, 3 - 3 * y_side, 1, keepdims=False), 4)
    layers = jnp.concatenate([wider, y_face[:, None]], axis=1).reshape(2, 25, 8, coeffs)
    place = lambda z, xy: (z & 1) + 2 * xy + 8 * (z >> 1)
    ups = [(place(z, xy), place(z + 1, xy)) for z in range(3) for xy in range(4)]
    below = lax.ppermute(layers[1], "sub", ups)
    above = lax.ppermute(layers[0], "sub", [(j, i) for i, j in ups])
    return (own, x_face.reshape(8, 8, coeffs), y_face.reshape(10, 8, coeffs), below, above, mirror)


def shards(points, forces, counts, droplet, contrast, ulist, vlist0, vlist1, vlist2,
           wave, phases, p2m_mix, m2m, m2l, l2l, l2p_mix):
    both = ("grp", "sub")
    leaves = counts.shape[0]
    coeffs = m2l.shape[1]
    devices = lax.axis_size(both)
    device = lax.axis_index(both)
    first = device * leaves
    first_arg = first.astype(jnp.int32).reshape(1)

    ids = (first + jnp.arange(leaves * PTS, dtype=jnp.int32) // PTS).astype(F32)[None, :]
    slots = jnp.concatenate([points, forces, droplet.astype(F32)[None, :], ids], axis=0)

    width = HALO * PTS
    count_row = jnp.repeat(counts, PTS).astype(F32)[None, :]

    def edge(part):
        return jnp.concatenate([slots[0:6, part], count_row[:, part], slots[7:8, part]], axis=0)

    right_way = [(i, i + 1) for i in range(devices - 1)]
    left_way = [(i + 1, i) for i in range(devices - 1)]
    left = lax.ppermute(edge(slice(leaves * PTS - width, None)), both, right_way)
    right = lax.ppermute(edge(slice(0, width)), both, left_way)
    left_counts = left[6].reshape(HALO, PTS)[:, 0].astype(jnp.int32)
    right_counts = right[6].reshape(HALO, PTS)[:, 0].astype(jnp.int32)

    turns = 1.0 / (2.0 * math.pi)
    columns = -(-2 * coeffs // LANES) * LANES
    first_half = ((0, 0), (0, columns - coeffs))
    constants = jnp.concatenate(
        [
            jnp.pad(wave * turns, first_half),
            jnp.pad(p2m_mix, ((0, 0), (coeffs, columns - 2 * coeffs))),
            jnp.zeros((2, columns), F32),
            jnp.pad(phases * turns, ((0, 6), first_half[1])),
            jnp.pad(l2p_mix, ((0, 5), first_half[1])),
        ],
        axis=0,
    )
    packed, leaf_mult, up = upward_pass(first_arg, counts, slots, constants, m2m)

    mid, top = leaves // 8, leaves // 64
    upper = lax.all_gather(up, both, axis=0, tiled=True).reshape(-1, 8, coeffs)
    pieces = leaf_pieces(leaf_mult.reshape(mid, 8, coeffs), lax.axis_index("sub"))

    local_list = jnp.where(ulist >= 0, ulist - first + HALO, -1)
    near = near_field(first_arg, counts, left_counts, right_counts, packed, left, right, local_list)

    rows0 = first + jnp.arange(leaves, dtype=jnp.int32)
    rows1 = device * mid + jnp.arange(mid, dtype=jnp.int32)
    rows2 = device * top + jnp.arange(top, dtype=jnp.int32)
    places = jnp.concatenate(
        [
            list_places(vlist0, rows0 >> 3, ROOT_BITS - 1),
            list_places(vlist1, rows1 >> 3, ROOT_BITS - 2),
            jnp.pad(list_places(vlist2, rows2 >> 3, ROOT_BITS - 3), ((0, 8 - top), (0, 0)), constant_values=-1),
        ],
        axis=0,
    )
    of_parents = upper_blocks(device * top + jnp.arange(top, dtype=jnp.int32), ROOT_BITS - 2, devices * top)
    of_tops = upper_blocks((device * top >> 3).reshape(1), ROOT_BITS - 3, devices * top // 8)
    blocks = jnp.concatenate(
        [
            leaf_blocks(),
            (of_parents >> 2) * 5 + (of_parents & 3),
            of_tops * 10 + 4,
        ],
        axis=0,
    )
    return far_field(first_arg, counts, blocks, places, pieces, upper, m2l, l2l, packed, near,
                     constants, contrast[None, :])


def solution(mesh):
    spread = P(("grp", "sub"))
    rows = P(("grp", "sub"), None)
    columns = P(None, ("grp", "sub"))
    return jax.shard_map(
        shards,
        mesh=mesh,
        in_specs=(
            columns, columns, spread, spread, P(), rows, rows, rows, rows,
            P(), P(), P(), P(), P(), P(), P(),
        ),
        out_specs=columns,
        check_vma=False,
    )
```

```python
import functools
import math

import jax
import jax.numpy as jnp
from jax import lax
from jax.experimental import pallas as pl
from jax.experimental.pallas import tpu as pltpu
from jax.sharding import PartitionSpec as P

PTS = 64
HALO = 16
EPS_SQ = 0.3 * 0.3
LANES = 128
NEIGHBOURS = 27
ROOT_BITS = 5
TURNS = 1.0 / (2.0 * math.pi)

F32 = jnp.float32
BF16 = jnp.bfloat16

COS_COEFFS = (
    0.9999999890590235,
    -19.739204499453994,
    64.93911745989843,
    -85.45013953092186,
    60.167630951185615,
    -25.967599249120923,
    6.528658161956132,
)

NT = (((1,), (1,)), ((), ()))
NN = (((1,), (0,)), ((), ()))


def params(megabytes):
    return pltpu.CompilerParams(vmem_limit_bytes=megabytes * 1024 * 1024)


def dot(left, right, dims=NN):
    return lax.dot_general(left, right, dims, preferred_element_type=F32)


def kernel_split3(value):
    high = value.astype(BF16).astype(F32)
    rest = value - high
    middle = rest.astype(BF16).astype(F32)
    return high, middle, rest - middle


def kernel_split2(value):
    high = value.astype(BF16)
    return high, (value - high.astype(F32)).astype(BF16)


def stack_rows(pieces, rows, start=0):
    shape = (rows, pieces[0].shape[1])
    row = lax.broadcasted_iota(jnp.int32, shape, 0)
    result = jnp.zeros(shape, F32)
    for k, piece in enumerate(pieces):
        result = jnp.where(row == start + k, jnp.broadcast_to(piece, shape), result)
    return result


def parameter_rows(ref, first, last, start=0, scale=1.0):
    rows = stack_rows([ref[k:k + 1, :] * scale for k in range(first, last)], 8, start)
    pad = -rows.shape[1] % LANES
    return jnp.concatenate([rows, jnp.zeros((8, pad), F32)], axis=1)


def weight_pieces(matrix, bias):
    high, middle, low = kernel_split3(matrix)
    shift = stack_rows(kernel_split3(bias), 8)
    pieces = [high, high, middle, middle, high, low, shift]
    pieces.append(jnp.zeros((LANES - 56, matrix.shape[1]), F32))
    return jnp.transpose(jnp.concatenate(pieces, axis=0))[:, :64].astype(BF16)


def feature_pieces(rows):
    high, middle, low = kernel_split3(rows)
    ones = jnp.where(lax.broadcasted_iota(jnp.int32, rows.shape, 0) < 3, 1.0, 0.0)
    pieces = [high, middle, high, middle, low, high, ones, jnp.zeros_like(rows)]
    return jnp.concatenate(pieces, axis=0).astype(BF16)


def cos_turns(turns):
    part = turns - jnp.round(turns)
    square = part * part
    value = jnp.full_like(square, COS_COEFFS[-1])
    for coeff in COS_COEFFS[-2::-1]:
        value = value * square + coeff
    return value


def center_rows(ids):
    axis = lax.broadcasted_iota(jnp.int32, ids.shape, 0)
    total = jnp.zeros_like(ids)
    for bit in range(ROOT_BITS):
        total = total + (((ids >> (axis + 3 * bit)) & 1) << bit)
    return total.astype(F32) + 0.5


def block_features(block):
    row = lax.broadcasted_iota(jnp.int32, block.shape, 0)
    ids = block[7:8, :].astype(jnp.int32)
    centers = center_rows(jnp.broadcast_to(jnp.maximum(ids, 0), block.shape))
    rows = jnp.where(row < 3, block - centers, jnp.where(row < 6, block, 0.0))
    return rows, ids


def wide_features(packed_ref, block, first):
    pieces, leaves = [], []
    for step in range(2):
        rows, ids = block_features(packed_ref[block + step])
        pieces.append(feature_pieces(rows))
        leaves.append(ids - first)
    return jnp.concatenate(pieces, axis=1), jnp.concatenate(leaves, axis=1)


def pack_leaves(read_pair, count_of, pairs, dest, start, current):
    lane = lax.broadcasted_iota(jnp.int32, (8, LANES), 1)

    def body(part, carry):
        offset, held = carry
        for inner in range(8):
            pair = part * 8 + inner
            value = read_pair(pair)
            for half in range(2):
                count = count_of(2 * pair + half)
                block, place = offset >> 7, offset & 127
                rolled = pltpu.roll(value, (place + 64 * half) & 127, 1)
                merged = jnp.where(lane >= place, rolled, held)
                dest[block] = merged
                held = jnp.where(place + count >= LANES, rolled, merged)
                offset = offset + count
        return offset, held

    offset, held = lax.fori_loop(0, pairs // 8, body, (start, current))
    dest[offset >> 7] = held
    return offset


def finish_pack(dest, end, more):
    lane = lax.broadcasted_iota(jnp.int32, (8, LANES), 1)
    row = lax.broadcasted_iota(jnp.int32, (8, LANES), 0)
    block, place = end >> 7, end & 127
    empty = jnp.where(row == 7, -1.0, 0.0)
    dest[block] = jnp.where(lane >= place, empty, dest[block])
    for step in range(more):
        dest[block + 1 + step] = empty


def space_order(parent):
    x0, y0, z0, x1, y1 = ((parent >> bit) & 1 for bit in range(5))
    return (z0 * 4 + y1 * 2 + y0) * 4 + x1 * 2 + x0


def upward_kernel(coeffs, base_ref, counts_ref, slots_ref, wave_ref, phases_ref, mix_ref, m2m_ref,
                  packed_ref, leaf_ref, up_ref, acc, staged, parents, weights, mix_weights):
    leaves = counts_ref.shape[0]
    lane = lax.broadcasted_iota(jnp.int32, (8, LANES), 1)

    def read_pair(pair):
        return slots_ref[:, pl.ds(pl.multiple_of(pair * LANES, LANES), LANES)]

    total = pack_leaves(
        read_pair, lambda leaf: counts_ref[leaf], leaves // 2, packed_ref,
        jnp.int32(0), jnp.zeros((8, LANES), F32),
    )
    finish_pack(packed_ref, total, 3)
    bias = parameter_rows(phases_ref, 0, 1, 0, TURNS)[0:1, :]
    weights[...] = weight_pieces(parameter_rows(wave_ref, 0, 3, 0, TURNS), bias)
    mix_weights[...] = weight_pieces(parameter_rows(mix_ref, 0, 3, 3), jnp.zeros_like(bias))
    acc[...] = jnp.zeros_like(acc)
    first = base_ref[0]

    def body(part, carry):
        left_side, right_side = [], []
        for inner in range(2):
            features, local = wide_features(packed_ref, part * 4 + inner * 2, first)
            turns = dot(weights[0:coeffs, :], features)
            high, low = kernel_split2(cos_turns(turns) * dot(mix_weights[0:coeffs, :], features))
            hits = lax.broadcasted_iota(jnp.int32, (leaves, 2 * LANES), 0) == local
            which = jnp.where(hits, 1.0, 0.0).astype(BF16)
            left_side += [which, which]
            right_side += [high, low]
        acc[...] += dot(jnp.concatenate(left_side, axis=1), jnp.concatenate(right_side, axis=1), NT)
        return carry

    lax.fori_loop(0, (total + 4 * LANES - 1) >> 9, body, 0)
    leaf = acc[...].astype(BF16)
    leaf_f32 = leaf.astype(F32)
    for parent in range(leaves // 8):
        place = 8 * space_order(parent)
        acc[place:place + 8, :] = leaf_f32[8 * parent:8 * parent + 8, :]
    leaf_ref[...] = acc[...].astype(BF16)
    tiles = staged.shape[0]

    def stage(target, value):
        for tile in range(tiles):
            low_col = tile * LANES
            width = min(LANES, coeffs - low_col)
            target[tile, :, :width] = value[:, low_col:low_col + width]

    def child(source, which, rows):
        parts = [source[tile, pl.ds(which, rows, stride=8), :] for tile in range(tiles)]
        return jnp.concatenate(parts, axis=1)[:, :coeffs].astype(BF16)

    stage(staged, leaf_f32)
    above = jnp.zeros((leaves // 8, coeffs), F32)
    for which in range(8):
        above = above + dot(child(staged, which, leaves // 8), m2m_ref[which])
    up = above.astype(BF16)
    stage(parents, up.astype(F32))
    top = jnp.zeros((leaves // 64, coeffs), F32)
    for which in range(8):
        top = top + dot(child(parents, which, leaves // 64), m2m_ref[which])
    half = jnp.zeros_like(top)
    odd = ((first // leaves) & 1) == 1
    block = jnp.concatenate([jnp.where(odd, half, top), jnp.where(odd, top, half)], axis=0)
    up_ref[...] = jnp.concatenate([above, block], axis=0).astype(BF16)


def upward_pass(first_leaf, counts, slots, wave, phases, mix, m2m):
    leaves, coeffs = counts.shape[0], m2m.shape[1]
    blocks = slots.shape[1] // LANES
    tiles = -(-coeffs // LANES)
    smem = pl.BlockSpec(memory_space=pltpu.SMEM)
    vmem = pl.BlockSpec(memory_space=pltpu.VMEM)
    up_rows = leaves // 8 + 8
    return pl.pallas_call(
        functools.partial(upward_kernel, coeffs),
        out_shape=(
            jax.ShapeDtypeStruct((blocks + 4, 8, LANES), F32),
            jax.ShapeDtypeStruct((leaves, coeffs), BF16),
            jax.ShapeDtypeStruct((up_rows, coeffs), BF16),
        ),
        in_specs=[smem, smem] + [vmem] * 5,
        out_specs=(vmem, vmem, vmem),
        scratch_shapes=[
            pltpu.VMEM((leaves, coeffs), F32),
            pltpu.VMEM((tiles, leaves, LANES), F32),
            pltpu.VMEM((tiles, leaves // 8, LANES), F32),
            pltpu.VMEM((tiles * LANES, 64), BF16),
            pltpu.VMEM((tiles * LANES, 64), BF16),
        ],
        compiler_params=params(32),
        name="upward",
    )(first_leaf, counts, slots, wave, phases, mix, m2m)


def near_kernel(base_ref, counts_ref, left_counts, right_counts, packed_ref, left_ref, right_ref,
                ulist_ref, near_ref, sources, which_source, lists, shares, columns,
                targets, share_first, share_second, share_b, acc, starts, lows, highs):
    leaves = counts_ref.shape[0]
    window = leaves + 2 * HALO
    halo_blocks = HALO * PTS // LANES
    first = base_ref[0]
    lane = lax.broadcasted_iota(jnp.int32, (8, LANES), 1)
    row = lax.broadcasted_iota(jnp.int32, (8, LANES), 0)
    empty = jnp.where(row == 7, -1.0, 0.0)

    left_total = jnp.int32(0)
    for leaf in range(HALO):
        left_total = left_total + left_counts[leaf]
    left_start = HALO * PTS - left_total

    def note_left(leaf, offset):
        starts[leaf] = offset
        return offset + left_counts[leaf]

    offset = lax.fori_loop(0, HALO, note_left, left_start)

    def note_own(leaf, offset):
        starts[HALO + leaf] = offset
        return offset + counts_ref[leaf]

    own_end = lax.fori_loop(0, leaves, note_own, offset)

    def note_right(leaf, offset):
        starts[HALO + leaves + leaf] = offset
        return offset + right_counts[leaf]

    end = lax.fori_loop(0, HALO, note_right, own_end)
    starts[window] = end

    def pair_of(ref):
        return lambda pair: ref[:, pl.ds(pl.multiple_of(pair * LANES, LANES), LANES)]

    pack_leaves(pair_of(left_ref), lambda leaf: left_counts[leaf], HALO // 2, sources, left_start, empty)
    own_blocks = (own_end - HALO * PTS + LANES - 1) >> 7

    def copy_block(block, carry):
        sources[halo_blocks + block] = packed_ref[block]
        return carry

    lax.fori_loop(0, own_blocks, copy_block, 0)
    held = sources[own_end >> 7]
    pack_leaves(pair_of(right_ref), lambda leaf: right_counts[leaf], HALO // 2, sources, own_end, held)
    finish_pack(sources, end, 3)

    own_list = ulist_ref[...]
    own_list = jnp.where(own_list >= 0, own_list - first + HALO, -1)
    column = lax.broadcasted_iota(jnp.int32, (leaves, window), 1)
    times = jnp.zeros((leaves, window), F32)
    for slot in range(own_list.shape[1]):
        times = times + jnp.where(own_list[:, slot:slot + 1] == column, 1.0, 0.0)
    lists[...] = times.astype(BF16)

    def mark_source(tile, carry):
        ids = sources[tile][7:8, :].astype(jnp.int32)
        local = jnp.broadcast_to(jnp.where(ids < 0, -1, ids - first + HALO), (window, LANES))
        hits = lax.broadcasted_iota(jnp.int32, (window, LANES), 0) == local
        which_source[tile] = jnp.where(hits, 1.0, 0.0).astype(BF16)
        return carry

    lax.fori_loop(left_start >> 7, (end >> 7) + 4, mark_source, 0)

    def mark_targets(part, carry):
        for inner in range(4):
            block = part * 4 + inner
            padded = jnp.concatenate([packed_ref[block], jnp.zeros((LANES - 8, LANES), F32)], axis=0)
            turned = jnp.transpose(padded)
            columns[block] = turned
            ids = turned[:, 7:8].astype(jnp.int32) - first
            hits = lax.broadcasted_iota(jnp.int32, (LANES, leaves), 1) == ids
            shares[block] = dot(jnp.where(hits, 1.0, 0.0).astype(BF16), lists[...]).astype(BF16)
            live = padded[7:8, :]
            low_leaf = jnp.min(jnp.where(live < 0.0, 1e9, live)).astype(jnp.int32) - first
            high_leaf = jnp.max(live).astype(jnp.int32) - first
            low = starts[jnp.clip(low_leaf, 0, leaves - 1)] >> 7
            high = (starts[jnp.clip(high_leaf, 0, leaves - 1) + 2 * HALO + 1] + LANES - 1) >> 7
            lows[block] = jnp.where(block < own_blocks, low, halo_blocks)
            highs[block] = jnp.where(block < own_blocks, high, halo_blocks)
        return carry

    lax.fori_loop(0, (own_blocks + 3) >> 2, mark_targets, 0)
    ones = jnp.ones((8, 2 * LANES), BF16)

    def close_blocks(pair):
        for which in range(2):
            rows = []
            for axis in range(3):
                high, low = kernel_split2(acc[pair & 1, which, axis])
                rows.append(dot(ones, jnp.concatenate([high, low], axis=1), NT)[0:1, :])
            near_ref[2 * pair + which] = stack_rows(rows, 8) * (1.0 / (8.0 * math.pi))

    def target_blocks(pair, carry):
        close_blocks(jnp.maximum(pair - 1, 0))
        now = pair & 1
        acc[now] = jnp.zeros(acc.shape[1:], F32)
        for which, share_a in enumerate((share_first, share_second)):
            turned = columns[2 * pair + which]
            for axis in range(3):
                targets[which, axis] = jnp.broadcast_to(turned[:, axis:axis + 1], (LANES, LANES))
            share_a[...] = dot(shares[2 * pair + which], which_source[lows[2 * pair + which]])

        for which, share_a in enumerate((share_first, share_second)):
            block = 2 * pair + which
            source_low, source_high = lows[block], highs[block]

            def source_tile(tile, share, which=which):
                value = sources[tile]
                feature = [jnp.broadcast_to(value[k:k + 1, :], (8, LANES)) for k in range(6)]
                for chunk in range(LANES // 8):
                    span = slice(8 * chunk, 8 * chunk + 8)
                    dx = targets[which, 0, span, :] - feature[0]
                    dy = targets[which, 1, span, :] - feature[1]
                    dz = targets[which, 2, span, :] - feature[2]
                    dist_sq = dx * dx + dy * dy + (dz * dz + EPS_SQ)
                    along = dx * feature[3] + dy * feature[4] + dz * feature[5]
                    inverse = lax.rsqrt(dist_sq)
                    weighted = share[span, :] * inverse
                    cubed = weighted * (inverse * inverse)
                    plain = weighted + EPS_SQ * cubed
                    outer = along * cubed
                    acc[now, which, 0, span, :] += plain * feature[3] + outer * dx
                    acc[now, which, 1, span, :] += plain * feature[4] + outer * dy
                    acc[now, which, 2, span, :] += plain * feature[5] + outer * dz

            def two_tiles(part, carry, block=block, low=source_low, share_a=share_a, source_tile=source_tile):
                tile = low + 2 * part
                share_b[...] = dot(shares[block], which_source[tile + 1])
                source_tile(tile, share_a)
                share_a[...] = dot(shares[block], which_source[tile + 2])
                source_tile(tile + 1, share_b)
                return carry

            lax.fori_loop(0, (source_high - source_low) >> 1, two_tiles, 0)

            @pl.when(((source_high - source_low) & 1) == 1)
            def _(high=source_high, share_a=share_a, source_tile=source_tile):
                source_tile(high - 1, share_a)

        return carry

    pairs = (own_blocks + 1) >> 1
    lax.fori_loop(0, pairs, target_blocks, 0)
    close_blocks(pairs - 1)


def near_field(first_leaf, counts, left_counts, right_counts, packed, left, right, ulist):
    leaves = counts.shape[0]
    window = leaves + 2 * HALO
    blocks = packed.shape[0]
    source_blocks = (leaves + 2 * HALO) * PTS // LANES + 4
    smem = pl.BlockSpec(memory_space=pltpu.SMEM)
    vmem = pl.BlockSpec(memory_space=pltpu.VMEM)
    return pl.pallas_call(
        near_kernel,
        out_shape=jax.ShapeDtypeStruct((blocks, 8, LANES), F32),
        in_specs=[smem] * 4 + [vmem] * 4,
        out_specs=vmem,
        scratch_shapes=[
            pltpu.VMEM((source_blocks, 8, LANES), F32),
            pltpu.VMEM((source_blocks, window, LANES), BF16),
            pltpu.VMEM((leaves, window), BF16),
            pltpu.VMEM((blocks + 2, LANES, window), BF16),
            pltpu.VMEM((blocks + 2, LANES, LANES), F32),
            pltpu.VMEM((2, 3, LANES, LANES), F32),
            pltpu.VMEM((LANES, LANES), F32),
            pltpu.VMEM((LANES, LANES), F32),
            pltpu.VMEM((LANES, LANES), F32),
            pltpu.VMEM((2, 2, 3, LANES, LANES), F32),
            pltpu.SMEM((window + 1,), jnp.int32),
            pltpu.SMEM((blocks,), jnp.int32),
            pltpu.SMEM((blocks,), jnp.int32),
        ],
        compiler_params=params(56),
        cost_estimate=pl.CostEstimate(flops=20_000_000_000, bytes_accessed=2_000_000, transcendentals=0),
        name="near_field",
    )(first_leaf, counts, left_counts, right_counts, packed, left, right, ulist)


def coords_of(code, bits):
    return [
        sum(((code >> (3 * bit + axis)) & 1) << bit for bit in range(bits)) for axis in range(3)
    ]


def code_of(coords, bits):
    return sum(
        ((coords[axis] >> bit) & 1) << (3 * bit + axis) for axis in range(3) for bit in range(bits)
    )


def list_places(vlist, parent_of_row, bits):
    own = coords_of(parent_of_row[:, None], bits)
    other = coords_of(vlist >> 3, bits)
    near = sum((o - m + 1) * 3 ** axis for axis, (o, m) in enumerate(zip(other, own)))
    slot = jnp.where(jnp.arange(vlist.shape[1])[None, :] == 0, NEIGHBOURS, near)
    return jnp.where(vlist >= 0, slot * 8 + (vlist & 7), -1)


def pool_steps():
    slot = jnp.arange(NEIGHBOURS + 1, dtype=jnp.int32)[None, :]
    return (slot % 3 - 1, slot // 3 % 3 - 1, slot // 9 % 3 - 1), slot == NEIGHBOURS


def upper_blocks(parents, bits, extent):
    steps, mirror = pool_steps()
    own = coords_of(parents[:, None], bits)
    code = code_of([jnp.clip(m + s, 0, 2 ** bits - 1) for m, s in zip(own, steps)], bits)
    return jnp.where(mirror, (parents[:, None] + extent // 2) % extent, code)


def leaf_blocks():
    steps, mirror = pool_steps()
    parent = jnp.arange(32, dtype=jnp.int32)[:, None]
    x = (parent & 1) + ((parent >> 3) & 1) * 2
    y = ((parent >> 1) & 1) + ((parent >> 4) & 1) * 2
    z = (parent >> 2) & 1
    at = (z * 4 + y) * 4 + x
    x, y, z = x + steps[0], y + steps[1], z + steps[2]
    x_out, y_out, z_out = (x < 0) | (x > 3), (y < 0) | (y > 3), (z < 0) | (z > 1)
    x, y = jnp.where(x_out, 4, x), jnp.where(y_out, 4, y)
    inside = jnp.where(
        y_out, 40 + z * 5 + x, jnp.where(x_out, 32 + z * 4 + y, (z * 4 + y) * 4 + x)
    )
    outside = jnp.where(z < 0, 50, 75) + y * 5 + x
    return jnp.where(mirror, 100 + at, jnp.where(z_out, outside, inside))


def far_kernel(coeffs, base_ref, counts_ref, blocks_ref, places_ref, *rest):
    (own_ref, x_ref, y_ref, below_ref, above_ref, mirror_ref, upper_table,
     m2l_hbm, l2l_ref, packed_ref, near_ref, wave_ref, phases_ref, mix_ref, contrast_ref, out_ref,
     gathered, table, pool, acc, m2l, local, leaf_local, spread, done, weights, sems) = rest
    leaves = counts_ref.shape[0]
    mid, top = leaves // 8, leaves // 64
    rows = places_ref.shape[0]
    slots = places_ref.shape[1]
    tiles = local.shape[0]
    first = base_ref[0]
    parts = sems.shape[0]
    share = slots // parts
    fetches = [
        pltpu.make_async_copy(m2l_hbm.at[pl.ds(k * share, share)], m2l.at[pl.ds(k * share, share)], sems.at[k])
        for k in range(parts)
    ]
    for fetch in fetches:
        fetch.start()
    weights[...] = weight_pieces(
        parameter_rows(wave_ref, 0, 3, 0, TURNS), parameter_rows(phases_ref, 1, 2, 0, TURNS)[0:1, :]
    )
    wide = lax.broadcasted_iota(jnp.int32, (8, pool.shape[1]), 1)

    filled = 0
    for piece in (own_ref, x_ref, y_ref, below_ref, above_ref, mirror_ref):
        table[filled:filled + piece.shape[0]] = piece[...].astype(F32)
        filled += piece.shape[0]

    def gather_from(source, width, halves):
        def body(part, carry):
            for inner in range(width):
                group = part * width + inner
                for slot in range(NEIGHBOURS + 1):
                    at = blocks_ref[group, slot]
                    value = source[at].astype(F32)
                    if halves:
                        value = value + source[at + 5].astype(F32)
                    pool[inner, 8 * slot:8 * slot + 8, :] = value
                start = pl.multiple_of(group * 8, 8)
                places = places_ref[pl.ds(start, 8), :]
                hits = [jnp.where(places[:, t:t + 1] == wide, 1.0, 0.0) for t in range(slots)]
                picked = dot(jnp.concatenate(hits, axis=0).astype(BF16), pool[inner].astype(BF16))
                for t in range(slots):
                    gathered[t, pl.ds(start, 8), :] = picked[8 * t:8 * t + 8, :]
            return carry

        return body

    lax.fori_loop(0, mid // 4, gather_from(table, 4, False), 0)
    lax.fori_loop(mid // 4, (mid + top) // 4, gather_from(upper_table, 4, False), 0)
    lax.fori_loop(mid + top, rows // 8, gather_from(upper_table, 1, True), 0)

    acc[...] = jnp.zeros_like(acc)
    step = 4

    def translate(part, carry):
        total = jnp.zeros((rows, coeffs), F32)
        for inner in range(step):
            t = part * step + inner
            total = total + dot(gathered[t].astype(BF16), m2l[t])
        acc[...] += total
        return carry

    for k, fetch in enumerate(fetches):
        fetch.wait()
        lax.fori_loop(k * share // step, (k + 1) * share // step, translate, 0)

    def spread_down(value, count):
        for which in range(8):
            child = dot(value, l2l_ref[which])
            for tile in range(tiles):
                low_col = tile * LANES
                width = min(LANES, coeffs - low_col)
                part = child[:count, low_col:low_col + width]
                if width < LANES:
                    part = jnp.concatenate([part, jnp.zeros((count, LANES - width), F32)], axis=1)
                local[tile, pl.ds(which, count, stride=8), :] = part
        return jnp.concatenate([local[tile, 0:8 * count, :] for tile in range(tiles)], axis=1)

    grand = acc[leaves + mid:, :] * 0.25
    middle = spread_down(grand.astype(BF16), top)[:, :coeffs] + acc[leaves:leaves + mid, :] * 0.5
    down = spread_down(middle.astype(BF16), mid)
    leaf_local[...] = down
    leaf_local[:, :coeffs] = down[:, :coeffs] + acc[0:leaves, :]
    flipped = jnp.transpose(leaf_local[...])[:coeffs, :]
    high, low = kernel_split2(flipped)
    spread[0:coeffs, :] = high
    spread[coeffs:, :] = low

    total = jnp.int32(0)

    def count_up(leaf, offset):
        return offset + counts_ref[leaf]

    total = lax.fori_loop(0, leaves, count_up, jnp.int32(0))

    mix_high, mix_low, _ = kernel_split3(stack_rows([mix_ref[k:k + 1, :] for k in range(3)], 8))
    mix = jnp.concatenate([mix_high, mix_low], axis=0).astype(BF16)
    factors = stack_rows(kernel_split3(2.0 / (1.0 + contrast_ref[0:1, :])), 16).astype(BF16)

    def evaluate(part, carry):
        for inner in range(2):
            block = part * 4 + inner * 2
            features, local_id = wide_features(packed_ref, block, first)
            turns = dot(weights[0:coeffs, :], features)
            hits = lax.broadcasted_iota(jnp.int32, (leaves, 2 * LANES), 0) == local_id
            both = dot(spread[...], jnp.where(hits, 1.0, 0.0).astype(BF16))
            product = cos_turns(turns) * (both[:coeffs] + both[coeffs:])
            high, low = kernel_split2(product)
            mixed, mixed_low = dot(mix, high), dot(mix, low)
            far = mixed[0:8] + (mixed[8:16] + mixed_low[0:8])
            drop = jnp.concatenate([packed_ref[block + step][6:7, :] for step in range(2)], axis=1)
            pick = lax.broadcasted_iota(jnp.int32, (factors.shape[1], 2 * LANES), 0) == drop.astype(jnp.int32)
            parts = dot(factors, jnp.where(pick, 1.0, 0.0).astype(BF16))
            factor = parts[0:1] + (parts[1:2] + parts[2:3])
            for step in range(2):
                span = slice(step * LANES, (step + 1) * LANES)
                done[block + step] = (near_ref[block + step] + far[:, span]) * factor[:, span]
        return carry

    lax.fori_loop(0, (total + 4 * LANES - 1) >> 9, evaluate, 0)

    lane = lax.broadcasted_iota(jnp.int32, (8, LANES), 1)

    def unpack(part, offset):
        for inner in range(8):
            pair = part * 8 + inner
            result = jnp.zeros((8, LANES), F32)
            for half in range(2):
                count = counts_ref[2 * pair + half]
                block, place = offset >> 7, offset & 127
                merged = jnp.where(lane >= place, done[block], done[block + 1])
                turned = pltpu.roll(merged, (64 * half - place) & 127, 1)
                result = jnp.where((lane >= 64 * half) & (lane < 64 * half + count), turned, result)
                offset = offset + count
            out_ref[:, pl.ds(pl.multiple_of(pair * LANES, LANES), LANES)] = result[0:3, :]
        return offset

    lax.fori_loop(0, leaves // 16, unpack, jnp.int32(0))


def far_field(first_leaf, counts, blocks, places, pieces, upper, m2l, l2l, packed, near,
              wave, phases, mix, contrast):
    leaves, coeffs = counts.shape[0], m2l.shape[1]
    tiles = -(-coeffs // LANES)
    rows = places.shape[0]
    table_blocks = sum(piece.shape[0] for piece in pieces)
    smem = pl.BlockSpec(memory_space=pltpu.SMEM)
    vmem = pl.BlockSpec(memory_space=pltpu.VMEM)
    anywhere = pl.BlockSpec(memory_space=pl.ANY)
    return pl.pallas_call(
        functools.partial(far_kernel, coeffs),
        out_shape=jax.ShapeDtypeStruct((3, leaves * PTS), F32),
        in_specs=[smem] * 3 + [vmem] * 8 + [anywhere] + [vmem] * 7,
        out_specs=vmem,
        scratch_shapes=[
            pltpu.VMEM((m2l.shape[0], rows, coeffs), F32),
            pltpu.VMEM((table_blocks, 8, coeffs), F32),
            pltpu.VMEM((4, (NEIGHBOURS + 1) * 8, coeffs), F32),
            pltpu.VMEM((rows, coeffs), F32),
            pltpu.VMEM(m2l.shape, BF16),
            pltpu.VMEM((tiles, leaves, LANES), F32),
            pltpu.VMEM((leaves, tiles * LANES), F32),
            pltpu.VMEM((2 * coeffs, leaves), BF16),
            pltpu.VMEM(packed.shape, F32),
            pltpu.VMEM((tiles * LANES, 64), BF16),
            pltpu.SemaphoreType.DMA((5,)),
        ],
        compiler_params=params(60),
        name="far_field",
    )(first_leaf, counts, blocks, places, *pieces, upper, m2l, l2l, packed, near, wave, phases, mix, contrast)


def leaf_pieces(own, sub):
    coeffs = own.shape[2]
    box = own.reshape(2, 4, 4, 8, coeffs)
    x_side, y_side = (sub >> 1) & 1, (sub >> 2) & 1
    swap = lambda value, bit: lax.ppermute(value, "sub", [(i, i ^ bit) for i in range(16)])
    mirror = swap(own, 8)
    x_face = swap(lax.dynamic_index_in_dim(box, 3 - 3 * x_side, 2, keepdims=False), 2)
    wider = jnp.concatenate([box, x_face[:, :, None]], axis=2)
    y_face = swap(lax.dynamic_index_in_dim(wider, 3 - 3 * y_side, 1, keepdims=False), 4)
    layers = jnp.concatenate([wider, y_face[:, None]], axis=1).reshape(2, 25, 8, coeffs)
    place = lambda z, xy: (z & 1) + 2 * xy + 8 * (z >> 1)
    ups = [(place(z, xy), place(z + 1, xy)) for z in range(3) for xy in range(4)]
    below = lax.ppermute(layers[1], "sub", ups)
    above = lax.ppermute(layers[0], "sub", [(j, i) for i, j in ups])
    return (own, x_face.reshape(8, 8, coeffs), y_face.reshape(10, 8, coeffs), below, above, mirror)


def shards(points, forces, counts, droplet, contrast, ulist, vlist0, vlist1, vlist2,
           wave, phases, p2m_mix, m2m, m2l, l2l, l2p_mix):
    both = ("grp", "sub")
    leaves = counts.shape[0]
    coeffs = m2l.shape[1]
    devices = lax.axis_size(both)
    device = lax.axis_index(both)
    first = device * leaves
    first_arg = first.astype(jnp.int32).reshape(1)

    ids = (first + jnp.arange(leaves * PTS, dtype=jnp.int32) // PTS).astype(F32)[None, :]
    slots = jnp.concatenate([points, forces, droplet.astype(F32)[None, :], ids], axis=0)

    width = HALO * PTS
    count_row = jnp.repeat(counts, PTS).astype(F32)[None, :]

    def edge(part):
        return jnp.concatenate([slots[0:6, part], count_row[:, part], slots[7:8, part]], axis=0)

    packed, leaf_mult, up = upward_pass(first_arg, counts, slots, wave, phases, p2m_mix, m2m)

    mid, top = leaves // 8, leaves // 64
    upper = lax.all_gather(up, both, axis=0, tiled=True).reshape(-1, 8, coeffs)
    pieces = leaf_pieces(leaf_mult.reshape(mid, 8, coeffs), lax.axis_index("sub"))

    last, head = edge(slice(leaves * PTS - width, None)), edge(slice(0, width))
    last, head, packed = lax.optimization_barrier((last, head, packed))
    right_way = [(i, i + 1) for i in range(devices - 1)]
    left_way = [(i + 1, i) for i in range(devices - 1)]
    left = lax.ppermute(last, both, right_way)
    right = lax.ppermute(head, both, left_way)
    left_counts = left[6].reshape(HALO, PTS)[:, 0].astype(jnp.int32)
    right_counts = right[6].reshape(HALO, PTS)[:, 0].astype(jnp.int32)

    near = near_field(first_arg, counts, left_counts, right_counts, packed, left, right, ulist)

    rows0 = first + jnp.arange(leaves, dtype=jnp.int32)
    rows1 = device * mid + jnp.arange(mid, dtype=jnp.int32)
    rows2 = device * top + jnp.arange(top, dtype=jnp.int32)
    places = jnp.concatenate(
        [
            list_places(vlist0, rows0 >> 3, ROOT_BITS - 1),
            list_places(vlist1, rows1 >> 3, ROOT_BITS - 2),
            jnp.pad(list_places(vlist2, rows2 >> 3, ROOT_BITS - 3), ((0, 8 - top), (0, 0)), constant_values=-1),
        ],
        axis=0,
    )
    of_parents = upper_blocks(device * top + jnp.arange(top, dtype=jnp.int32), ROOT_BITS - 2, devices * top)
    of_tops = upper_blocks((device * top >> 3).reshape(1), ROOT_BITS - 3, devices * top // 8)
    blocks = jnp.concatenate(
        [
            leaf_blocks(),
            (of_parents >> 2) * 5 + (of_parents & 3),
            of_tops * 10 + 4,
        ],
        axis=0,
    )
    return far_field(first_arg, counts, blocks, places, pieces, upper, m2l, l2l, packed, near,
                     wave, phases, l2p_mix, contrast[None, :])


def solution(mesh):
    spread = P(("grp", "sub"))
    rows = P(("grp", "sub"), None)
    columns = P(None, ("grp", "sub"))
    return jax.shard_map(
        shards,
        mesh=mesh,
        in_specs=(
            columns, columns, spread, spread, P(), rows, rows, rows, rows,
            P(), P(), P(), P(), P(), P(), P(),
        ),
        out_specs=columns,
        check_vma=False,
    )
```

```python
import functools
import math

import jax
import jax.numpy as jnp
from jax import lax
from jax.experimental import pallas as pl
from jax.experimental.pallas import tpu as pltpu
from jax.sharding import PartitionSpec as P

PTS = 64
HALO = 16
EPS_SQ = 0.3 * 0.3
LANES = 128
NEIGHBOURS = 27
ROOT_BITS = 5
TURNS = 1.0 / (2.0 * math.pi)

F32 = jnp.float32
BF16 = jnp.bfloat16

COS_COEFFS = (
    0.999999210782322,
    -19.738980355764046,
    64.92865742103419,
    -85.27162153430582,
    58.790492120148535,
    -21.07110562765538,
)

NT = (((1,), (1,)), ((), ()))
NN = (((1,), (0,)), ((), ()))


def params(megabytes):
    return pltpu.CompilerParams(vmem_limit_bytes=megabytes * 1024 * 1024)


def dot(left, right, dims=NN):
    return lax.dot_general(left, right, dims, preferred_element_type=F32)


def kernel_split3(value):
    high = value.astype(BF16).astype(F32)
    rest = value - high
    middle = rest.astype(BF16).astype(F32)
    return high, middle, rest - middle


def kernel_split2(value):
    high = value.astype(BF16)
    return high, (value - high.astype(F32)).astype(BF16)


def stack_rows(pieces, rows, start=0):
    shape = (rows, pieces[0].shape[1])
    row = lax.broadcasted_iota(jnp.int32, shape, 0)
    result = jnp.zeros(shape, F32)
    for k, piece in enumerate(pieces):
        result = jnp.where(row == start + k, jnp.broadcast_to(piece, shape), result)
    return result


def parameter_rows(ref, first, last, start=0, scale=1.0):
    rows = stack_rows([ref[k:k + 1, :] * scale for k in range(first, last)], 8, start)
    pad = -rows.shape[1] % LANES
    return jnp.concatenate([rows, jnp.zeros((8, pad), F32)], axis=1)


def weight_pieces(matrix, bias):
    high, middle, low = kernel_split3(matrix)
    shift = stack_rows(kernel_split3(bias), 8)
    pieces = [high, high, middle, middle, high, low, shift]
    pieces.append(jnp.zeros((LANES - 56, matrix.shape[1]), F32))
    return jnp.transpose(jnp.concatenate(pieces, axis=0))[:, :64].astype(BF16)


def feature_pieces(rows):
    high, middle, low = kernel_split3(rows)
    ones = jnp.where(lax.broadcasted_iota(jnp.int32, rows.shape, 0) < 3, 1.0, 0.0)
    pieces = [high, middle, high, middle, low, high, ones, jnp.zeros_like(rows)]
    return jnp.concatenate(pieces, axis=0).astype(BF16)


def cos_turns(turns):
    part = turns - jnp.round(turns)
    square = part * part
    value = jnp.full_like(square, COS_COEFFS[-1])
    for coeff in COS_COEFFS[-2::-1]:
        value = value * square + coeff
    return value


def center_rows(ids):
    axis = lax.broadcasted_iota(jnp.int32, ids.shape, 0)
    total = jnp.zeros_like(ids)
    for bit in range(ROOT_BITS):
        total = total + (((ids >> (axis + 3 * bit)) & 1) << bit)
    return total.astype(F32) + 0.5


def block_features(block):
    row = lax.broadcasted_iota(jnp.int32, block.shape, 0)
    ids = block[7:8, :].astype(jnp.int32)
    centers = center_rows(jnp.broadcast_to(jnp.maximum(ids, 0), block.shape))
    rows = jnp.where(row < 3, block - centers, jnp.where(row < 6, block, 0.0))
    return rows, ids


def wide_features(packed_ref, block, first):
    pieces, leaves = [], []
    for step in range(2):
        rows, ids = block_features(packed_ref[block + step])
        pieces.append(feature_pieces(rows))
        leaves.append(ids - first)
    return jnp.concatenate(pieces, axis=1), jnp.concatenate(leaves, axis=1)


def pack_leaves(read_pair, count_of, pairs, dest, start, current):
    lane = lax.broadcasted_iota(jnp.int32, (8, LANES), 1)

    def body(part, carry):
        offset, held = carry
        for inner in range(8):
            pair = part * 8 + inner
            value = read_pair(pair)
            for half in range(2):
                count = count_of(2 * pair + half)
                block, place = offset >> 7, offset & 127
                rolled = pltpu.roll(value, (place + 64 * half) & 127, 1)
                merged = jnp.where(lane >= place, rolled, held)
                dest[block] = merged
                held = jnp.where(place + count >= LANES, rolled, merged)
                offset = offset + count
        return offset, held

    offset, held = lax.fori_loop(0, pairs // 8, body, (start, current))
    dest[offset >> 7] = held
    return offset


def finish_pack(dest, end, more):
    lane = lax.broadcasted_iota(jnp.int32, (8, LANES), 1)
    row = lax.broadcasted_iota(jnp.int32, (8, LANES), 0)
    block, place = end >> 7, end & 127
    empty = jnp.where(row == 7, -1.0, 0.0)
    dest[block] = jnp.where(lane >= place, empty, dest[block])
    for step in range(more):
        dest[block + 1 + step] = empty


def space_order(parent):
    x0, y0, z0, x1, y1 = ((parent >> bit) & 1 for bit in range(5))
    return (z0 * 4 + y1 * 2 + y0) * 4 + x1 * 2 + x0


def upward_kernel(coeffs, base_ref, counts_ref, slots_ref, wave_ref, phases_ref, mix_ref, m2m_ref,
                  packed_ref, leaf_ref, up_ref, acc, staged, parents, weights, mix_weights):
    leaves = counts_ref.shape[0]
    lane = lax.broadcasted_iota(jnp.int32, (8, LANES), 1)

    def read_pair(pair):
        return slots_ref[:, pl.ds(pl.multiple_of(pair * LANES, LANES), LANES)]

    total = pack_leaves(
        read_pair, lambda leaf: counts_ref[leaf], leaves // 2, packed_ref,
        jnp.int32(0), jnp.zeros((8, LANES), F32),
    )
    finish_pack(packed_ref, total, 3)
    bias = parameter_rows(phases_ref, 0, 1, 0, TURNS)[0:1, :]
    weights[...] = weight_pieces(parameter_rows(wave_ref, 0, 3, 0, TURNS), bias)
    mix_weights[...] = weight_pieces(parameter_rows(mix_ref, 0, 3, 3), jnp.zeros_like(bias))
    acc[...] = jnp.zeros_like(acc)
    first = base_ref[0]

    def body(part, carry):
        left_side, right_side = [], []
        for inner in range(2):
            features, local = wide_features(packed_ref, part * 4 + inner * 2, first)
            turns = dot(weights[0:coeffs, :], features)
            high, low = kernel_split2(cos_turns(turns) * dot(mix_weights[0:coeffs, :], features))
            hits = lax.broadcasted_iota(jnp.int32, (leaves, 2 * LANES), 0) == local
            which = jnp.where(hits, 1.0, 0.0).astype(BF16)
            left_side += [which, which]
            right_side += [high, low]
        acc[...] += dot(jnp.concatenate(left_side, axis=1), jnp.concatenate(right_side, axis=1), NT)
        return carry

    lax.fori_loop(0, (total + 4 * LANES - 1) >> 9, body, 0)
    leaf = acc[...].astype(BF16)
    leaf_f32 = leaf.astype(F32)
    for parent in range(leaves // 8):
        place = 8 * space_order(parent)
        acc[place:place + 8, :] = leaf_f32[8 * parent:8 * parent + 8, :]
    leaf_ref[...] = acc[...].astype(BF16)
    tiles = staged.shape[0]

    def stage(target, value):
        for tile in range(tiles):
            low_col = tile * LANES
            width = min(LANES, coeffs - low_col)
            target[tile, :, :width] = value[:, low_col:low_col + width]

    def child(source, which, rows):
        parts = [source[tile, pl.ds(which, rows, stride=8), :] for tile in range(tiles)]
        return jnp.concatenate(parts, axis=1)[:, :coeffs].astype(BF16)

    stage(staged, leaf_f32)
    above = jnp.zeros((leaves // 8, coeffs), F32)
    for which in range(8):
        above = above + dot(child(staged, which, leaves // 8), m2m_ref[which])
    up = above.astype(BF16)
    stage(parents, up.astype(F32))
    top = jnp.zeros((leaves // 64, coeffs), F32)
    for which in range(8):
        top = top + dot(child(parents, which, leaves // 64), m2m_ref[which])
    half = jnp.zeros_like(top)
    odd = ((first // leaves) & 1) == 1
    block = jnp.concatenate([jnp.where(odd, half, top), jnp.where(odd, top, half)], axis=0)
    up_ref[...] = jnp.concatenate([above, block], axis=0).astype(BF16)


def upward_pass(first_leaf, counts, slots, wave, phases, mix, m2m):
    leaves, coeffs = counts.shape[0], m2m.shape[1]
    blocks = slots.shape[1] // LANES
    tiles = -(-coeffs // LANES)
    smem = pl.BlockSpec(memory_space=pltpu.SMEM)
    vmem = pl.BlockSpec(memory_space=pltpu.VMEM)
    up_rows = leaves // 8 + 8
    return pl.pallas_call(
        functools.partial(upward_kernel, coeffs),
        out_shape=(
            jax.ShapeDtypeStruct((blocks + 4, 8, LANES), F32),
            jax.ShapeDtypeStruct((leaves, coeffs), BF16),
            jax.ShapeDtypeStruct((up_rows, coeffs), BF16),
        ),
        in_specs=[smem, smem] + [vmem] * 5,
        out_specs=(vmem, vmem, vmem),
        scratch_shapes=[
            pltpu.VMEM((leaves, coeffs), F32),
            pltpu.VMEM((tiles, leaves, LANES), F32),
            pltpu.VMEM((tiles, leaves // 8, LANES), F32),
            pltpu.VMEM((tiles * LANES, 64), BF16),
            pltpu.VMEM((tiles * LANES, 64), BF16),
        ],
        compiler_params=params(32),
        name="upward",
    )(first_leaf, counts, slots, wave, phases, mix, m2m)


def near_kernel(base_ref, counts_ref, left_counts, right_counts, packed_ref, left_ref, right_ref,
                ulist_ref, near_ref, sources, which_source, lists, shares, columns,
                targets, share_first, share_second, share_b, acc, starts, lows, highs):
    leaves = counts_ref.shape[0]
    window = leaves + 2 * HALO
    halo_blocks = HALO * PTS // LANES
    first = base_ref[0]
    lane = lax.broadcasted_iota(jnp.int32, (8, LANES), 1)
    row = lax.broadcasted_iota(jnp.int32, (8, LANES), 0)
    empty = jnp.where(row == 7, -1.0, 0.0)

    left_total = jnp.int32(0)
    for leaf in range(HALO):
        left_total = left_total + left_counts[leaf]
    left_start = HALO * PTS - left_total

    def note_left(leaf, offset):
        starts[leaf] = offset
        return offset + left_counts[leaf]

    offset = lax.fori_loop(0, HALO, note_left, left_start)

    def note_own(leaf, offset):
        starts[HALO + leaf] = offset
        return offset + counts_ref[leaf]

    own_end = lax.fori_loop(0, leaves, note_own, offset)

    def note_right(leaf, offset):
        starts[HALO + leaves + leaf] = offset
        return offset + right_counts[leaf]

    end = lax.fori_loop(0, HALO, note_right, own_end)
    starts[window] = end

    def pair_of(ref):
        return lambda pair: ref[:, pl.ds(pl.multiple_of(pair * LANES, LANES), LANES)]

    pack_leaves(pair_of(left_ref), lambda leaf: left_counts[leaf], HALO // 2, sources, left_start, empty)
    own_blocks = (own_end - HALO * PTS + LANES - 1) >> 7

    def copy_block(block, carry):
        sources[halo_blocks + block] = packed_ref[block]
        return carry

    lax.fori_loop(0, own_blocks, copy_block, 0)
    held = sources[own_end >> 7]
    pack_leaves(pair_of(right_ref), lambda leaf: right_counts[leaf], HALO // 2, sources, own_end, held)
    finish_pack(sources, end, 3)

    own_list = ulist_ref[...]
    own_list = jnp.where(own_list >= 0, own_list - first + HALO, -1)
    column = lax.broadcasted_iota(jnp.int32, (leaves, window), 1)
    times = jnp.zeros((leaves, window), F32)
    for slot in range(own_list.shape[1]):
        times = times + jnp.where(own_list[:, slot:slot + 1] == column, 1.0, 0.0)
    lists[...] = times.astype(BF16)

    def mark_source(tile, carry):
        ids = sources[tile][7:8, :].astype(jnp.int32)
        local = jnp.broadcast_to(jnp.where(ids < 0, -1, ids - first + HALO), (window, LANES))
        hits = lax.broadcasted_iota(jnp.int32, (window, LANES), 0) == local
        which_source[tile] = jnp.where(hits, 1.0, 0.0).astype(BF16)
        return carry

    lax.fori_loop(left_start >> 7, (end >> 7) + 4, mark_source, 0)

    def mark_targets(part, carry):
        for inner in range(4):
            block = part * 4 + inner
            padded = jnp.concatenate([packed_ref[block], jnp.zeros((LANES - 8, LANES), F32)], axis=0)
            turned = jnp.transpose(padded)
            columns[block] = turned
            ids = turned[:, 7:8].astype(jnp.int32) - first
            hits = lax.broadcasted_iota(jnp.int32, (LANES, leaves), 1) == ids
            shares[block] = dot(jnp.where(hits, 1.0, 0.0).astype(BF16), lists[...]).astype(BF16)
            live = padded[7:8, :]
            low_leaf = jnp.min(jnp.where(live < 0.0, 1e9, live)).astype(jnp.int32) - first
            high_leaf = jnp.max(live).astype(jnp.int32) - first
            low = starts[jnp.clip(low_leaf, 0, leaves - 1)] >> 7
            high = (starts[jnp.clip(high_leaf, 0, leaves - 1) + 2 * HALO + 1] + LANES - 1) >> 7
            lows[block] = jnp.where(block < own_blocks, low, halo_blocks)
            highs[block] = jnp.where(block < own_blocks, high, halo_blocks)
        return carry

    lax.fori_loop(0, (own_blocks + 3) >> 2, mark_targets, 0)
    ones = jnp.ones((8, 2 * LANES), BF16)

    def close_blocks(pair):
        for which in range(2):
            rows = []
            for axis in range(3):
                high, low = kernel_split2(acc[pair & 1, which, axis])
                rows.append(dot(ones, jnp.concatenate([high, low], axis=1), NT)[0:1, :])
            near_ref[2 * pair + which] = stack_rows(rows, 8) * (1.0 / (8.0 * math.pi))

    def target_blocks(pair, carry):
        close_blocks(jnp.maximum(pair - 1, 0))
        now = pair & 1
        acc[now] = jnp.zeros(acc.shape[1:], F32)
        for which, share_a in enumerate((share_first, share_second)):
            turned = columns[2 * pair + which]
            for axis in range(3):
                targets[which, axis] = jnp.broadcast_to(turned[:, axis:axis + 1], (LANES, LANES))
            share_a[...] = dot(shares[2 * pair + which], which_source[lows[2 * pair + which]])

        for which, share_a in enumerate((share_first, share_second)):
            block = 2 * pair + which
            source_low, source_high = lows[block], highs[block]

            def source_tile(tile, share, which=which):
                value = sources[tile]
                feature = [jnp.broadcast_to(value[k:k + 1, :], (8, LANES)) for k in range(6)]
                for chunk in range(LANES // 8):
                    span = slice(8 * chunk, 8 * chunk + 8)
                    dx = targets[which, 0, span, :] - feature[0]
                    dy = targets[which, 1, span, :] - feature[1]
                    dz = targets[which, 2, span, :] - feature[2]
                    dist_sq = dx * dx + dy * dy + (dz * dz + EPS_SQ)
                    along = dx * feature[3] + dy * feature[4] + dz * feature[5]
                    inverse = lax.rsqrt(dist_sq)
                    weighted = share[span, :] * inverse
                    cubed = weighted * (inverse * inverse)
                    plain = weighted + EPS_SQ * cubed
                    outer = along * cubed
                    acc[now, which, 0, span, :] += plain * feature[3] + outer * dx
                    acc[now, which, 1, span, :] += plain * feature[4] + outer * dy
                    acc[now, which, 2, span, :] += plain * feature[5] + outer * dz

            def two_tiles(part, carry, block=block, low=source_low, share_a=share_a, source_tile=source_tile):
                tile = low + 2 * part
                share_b[...] = dot(shares[block], which_source[tile + 1])
                source_tile(tile, share_a)
                share_a[...] = dot(shares[block], which_source[tile + 2])
                source_tile(tile + 1, share_b)
                return carry

            lax.fori_loop(0, (source_high - source_low) >> 1, two_tiles, 0)

            @pl.when(((source_high - source_low) & 1) == 1)
            def _(high=source_high, share_a=share_a, source_tile=source_tile):
                source_tile(high - 1, share_a)

        return carry

    pairs = (own_blocks + 1) >> 1
    lax.fori_loop(0, pairs, target_blocks, 0)
    close_blocks(pairs - 1)


def near_field(first_leaf, counts, left_counts, right_counts, packed, left, right, ulist):
    leaves = counts.shape[0]
    window = leaves + 2 * HALO
    blocks = packed.shape[0]
    source_blocks = (leaves + 2 * HALO) * PTS // LANES + 4
    smem = pl.BlockSpec(memory_space=pltpu.SMEM)
    vmem = pl.BlockSpec(memory_space=pltpu.VMEM)
    return pl.pallas_call(
        near_kernel,
        out_shape=jax.ShapeDtypeStruct((blocks, 8, LANES), F32),
        in_specs=[smem] * 4 + [vmem] * 4,
        out_specs=vmem,
        scratch_shapes=[
            pltpu.VMEM((source_blocks, 8, LANES), F32),
            pltpu.VMEM((source_blocks, window, LANES), BF16),
            pltpu.VMEM((leaves, window), BF16),
            pltpu.VMEM((blocks + 2, LANES, window), BF16),
            pltpu.VMEM((blocks + 2, LANES, LANES), F32),
            pltpu.VMEM((2, 3, LANES, LANES), F32),
            pltpu.VMEM((LANES, LANES), F32),
            pltpu.VMEM((LANES, LANES), F32),
            pltpu.VMEM((LANES, LANES), F32),
            pltpu.VMEM((2, 2, 3, LANES, LANES), F32),
            pltpu.SMEM((window + 1,), jnp.int32),
            pltpu.SMEM((blocks,), jnp.int32),
            pltpu.SMEM((blocks,), jnp.int32),
        ],
        compiler_params=params(56),
        cost_estimate=pl.CostEstimate(flops=20_000_000_000, bytes_accessed=2_000_000, transcendentals=0),
        name="near_field",
    )(first_leaf, counts, left_counts, right_counts, packed, left, right, ulist)


def coords_of(code, bits):
    return [
        sum(((code >> (3 * bit + axis)) & 1) << bit for bit in range(bits)) for axis in range(3)
    ]


def code_of(coords, bits):
    return sum(
        ((coords[axis] >> bit) & 1) << (3 * bit + axis) for axis in range(3) for bit in range(bits)
    )


def list_places(vlist, parent_of_row, bits):
    own = coords_of(parent_of_row[:, None], bits)
    other = coords_of(vlist >> 3, bits)
    near = sum((o - m + 1) * 3 ** axis for axis, (o, m) in enumerate(zip(other, own)))
    slot = jnp.where(jnp.arange(vlist.shape[1])[None, :] == 0, NEIGHBOURS, near)
    return jnp.where(vlist >= 0, slot * 8 + (vlist & 7), -1)


def pool_steps():
    slot = jnp.arange(NEIGHBOURS + 1, dtype=jnp.int32)[None, :]
    return (slot % 3 - 1, slot // 3 % 3 - 1, slot // 9 % 3 - 1), slot == NEIGHBOURS


def upper_blocks(parents, bits, extent):
    steps, mirror = pool_steps()
    own = coords_of(parents[:, None], bits)
    code = code_of([jnp.clip(m + s, 0, 2 ** bits - 1) for m, s in zip(own, steps)], bits)
    return jnp.where(mirror, (parents[:, None] + extent // 2) % extent, code)


def leaf_blocks():
    steps, mirror = pool_steps()
    parent = jnp.arange(32, dtype=jnp.int32)[:, None]
    x = (parent & 1) + ((parent >> 3) & 1) * 2
    y = ((parent >> 1) & 1) + ((parent >> 4) & 1) * 2
    z = (parent >> 2) & 1
    at = (z * 4 + y) * 4 + x
    x, y, z = x + steps[0], y + steps[1], z + steps[2]
    x_out, y_out, z_out = (x < 0) | (x > 3), (y < 0) | (y > 3), (z < 0) | (z > 1)
    x, y = jnp.where(x_out, 4, x), jnp.where(y_out, 4, y)
    inside = jnp.where(
        y_out, 40 + z * 5 + x, jnp.where(x_out, 32 + z * 4 + y, (z * 4 + y) * 4 + x)
    )
    outside = jnp.where(z < 0, 50, 75) + y * 5 + x
    return jnp.where(mirror, 100 + at, jnp.where(z_out, outside, inside))


def far_kernel(coeffs, base_ref, counts_ref, blocks_ref, places_ref, *rest):
    (own_ref, x_ref, y_ref, below_ref, above_ref, mirror_ref, upper_table,
     m2l_hbm, l2l_ref, packed_ref, near_ref, wave_ref, phases_ref, mix_ref, contrast_ref, out_ref,
     gathered, table, pool, acc, m2l, local, leaf_local, spread, done, weights, sems) = rest
    leaves = counts_ref.shape[0]
    mid, top = leaves // 8, leaves // 64
    rows = places_ref.shape[0]
    slots = places_ref.shape[1]
    tiles = local.shape[0]
    first = base_ref[0]
    parts = sems.shape[0]
    share = slots // parts
    fetches = [
        pltpu.make_async_copy(m2l_hbm.at[pl.ds(k * share, share)], m2l.at[pl.ds(k * share, share)], sems.at[k])
        for k in range(parts)
    ]
    for fetch in fetches:
        fetch.start()
    weights[...] = weight_pieces(
        parameter_rows(wave_ref, 0, 3, 0, TURNS), parameter_rows(phases_ref, 1, 2, 0, TURNS)[0:1, :]
    )
    wide = lax.broadcasted_iota(jnp.int32, (8, pool.shape[1]), 1)

    filled = 0
    for piece in (own_ref, x_ref, y_ref, below_ref, above_ref, mirror_ref):
        table[filled:filled + piece.shape[0]] = piece[...].astype(F32)
        filled += piece.shape[0]

    def gather_from(source, width, halves):
        def body(part, carry):
            for inner in range(width):
                group = part * width + inner
                for slot in range(NEIGHBOURS + 1):
                    at = blocks_ref[group, slot]
                    value = source[at].astype(F32)
                    if halves:
                        value = value + source[at + 5].astype(F32)
                    pool[inner, 8 * slot:8 * slot + 8, :] = value
                start = pl.multiple_of(group * 8, 8)
                places = places_ref[pl.ds(start, 8), :]
                hits = [jnp.where(places[:, t:t + 1] == wide, 1.0, 0.0) for t in range(slots)]
                picked = dot(jnp.concatenate(hits, axis=0).astype(BF16), pool[inner].astype(BF16))
                for t in range(slots):
                    gathered[t, pl.ds(start, 8), :] = picked[8 * t:8 * t + 8, :]
            return carry

        return body

    lax.fori_loop(0, mid // 4, gather_from(table, 4, False), 0)
    lax.fori_loop(mid // 4, (mid + top) // 4, gather_from(upper_table, 4, False), 0)
    lax.fori_loop(mid + top, rows // 8, gather_from(upper_table, 1, True), 0)

    acc[...] = jnp.zeros_like(acc)
    step = 8

    def translate(part, carry):
        total = jnp.zeros((rows, coeffs), F32)
        for inner in range(step):
            t = part * step + inner
            total = total + dot(gathered[t].astype(BF16), m2l[t])
        acc[...] += total
        return carry

    for k, fetch in enumerate(fetches):
        fetch.wait()
        lax.fori_loop(k * share // step, (k + 1) * share // step, translate, 0)

    def spread_down(value, count):
        for which in range(8):
            child = dot(value, l2l_ref[which])
            for tile in range(tiles):
                low_col = tile * LANES
                width = min(LANES, coeffs - low_col)
                part = child[:count, low_col:low_col + width]
                if width < LANES:
                    part = jnp.concatenate([part, jnp.zeros((count, LANES - width), F32)], axis=1)
                local[tile, pl.ds(which, count, stride=8), :] = part
        return jnp.concatenate([local[tile, 0:8 * count, :] for tile in range(tiles)], axis=1)

    grand = acc[leaves + mid:, :] * 0.25
    middle = spread_down(grand.astype(BF16), top)[:, :coeffs] + acc[leaves:leaves + mid, :] * 0.5
    down = spread_down(middle.astype(BF16), mid)
    leaf_local[...] = down
    leaf_local[:, :coeffs] = down[:, :coeffs] + acc[0:leaves, :]
    flipped = jnp.transpose(leaf_local[...])[:coeffs, :]
    high, low = kernel_split2(flipped)
    spread[0:coeffs, :] = high
    spread[coeffs:, :] = low

    total = jnp.int32(0)

    def count_up(leaf, offset):
        return offset + counts_ref[leaf]

    total = lax.fori_loop(0, leaves, count_up, jnp.int32(0))

    mix_high, mix_low, _ = kernel_split3(stack_rows([mix_ref[k:k + 1, :] for k in range(3)], 8))
    mix = jnp.concatenate([mix_high, mix_low], axis=0).astype(BF16)
    factors = stack_rows(kernel_split3(2.0 / (1.0 + contrast_ref[0:1, :])), 16).astype(BF16)

    def evaluate(part, carry):
        for inner in range(2):
            block = part * 4 + inner * 2
            features, local_id = wide_features(packed_ref, block, first)
            turns = dot(weights[0:coeffs, :], features)
            hits = lax.broadcasted_iota(jnp.int32, (leaves, 2 * LANES), 0) == local_id
            both = dot(spread[...], jnp.where(hits, 1.0, 0.0).astype(BF16))
            product = cos_turns(turns) * (both[:coeffs] + both[coeffs:])
            high, low = kernel_split2(product)
            mixed, mixed_low = dot(mix, high), dot(mix, low)
            far = mixed[0:8] + (mixed[8:16] + mixed_low[0:8])
            drop = jnp.concatenate([packed_ref[block + step][6:7, :] for step in range(2)], axis=1)
            pick = lax.broadcasted_iota(jnp.int32, (factors.shape[1], 2 * LANES), 0) == drop.astype(jnp.int32)
            parts = dot(factors, jnp.where(pick, 1.0, 0.0).astype(BF16))
            factor = parts[0:1] + (parts[1:2] + parts[2:3])
            for step in range(2):
                span = slice(step * LANES, (step + 1) * LANES)
                done[block + step] = (near_ref[block + step] + far[:, span]) * factor[:, span]
        return carry

    lax.fori_loop(0, (total + 4 * LANES - 1) >> 9, evaluate, 0)

    lane = lax.broadcasted_iota(jnp.int32, (8, LANES), 1)

    def unpack(part, offset):
        for inner in range(8):
            pair = part * 8 + inner
            result = jnp.zeros((8, LANES), F32)
            for half in range(2):
                count = counts_ref[2 * pair + half]
                block, place = offset >> 7, offset & 127
                merged = jnp.where(lane >= place, done[block], done[block + 1])
                turned = pltpu.roll(merged, (64 * half - place) & 127, 1)
                result = jnp.where((lane >= 64 * half) & (lane < 64 * half + count), turned, result)
                offset = offset + count
            out_ref[:, pl.ds(pl.multiple_of(pair * LANES, LANES), LANES)] = result[0:3, :]
        return offset

    lax.fori_loop(0, leaves // 16, unpack, jnp.int32(0))


def far_field(first_leaf, counts, blocks, places, pieces, upper, m2l, l2l, packed, near,
              wave, phases, mix, contrast):
    leaves, coeffs = counts.shape[0], m2l.shape[1]
    tiles = -(-coeffs // LANES)
    rows = places.shape[0]
    table_blocks = sum(piece.shape[0] for piece in pieces)
    smem = pl.BlockSpec(memory_space=pltpu.SMEM)
    vmem = pl.BlockSpec(memory_space=pltpu.VMEM)
    anywhere = pl.BlockSpec(memory_space=pl.ANY)
    return pl.pallas_call(
        functools.partial(far_kernel, coeffs),
        out_shape=jax.ShapeDtypeStruct((3, leaves * PTS), F32),
        in_specs=[smem] * 3 + [vmem] * 8 + [anywhere] + [vmem] * 7,
        out_specs=vmem,
        scratch_shapes=[
            pltpu.VMEM((m2l.shape[0], rows, coeffs), F32),
            pltpu.VMEM((table_blocks, 8, coeffs), F32),
            pltpu.VMEM((4, (NEIGHBOURS + 1) * 8, coeffs), F32),
            pltpu.VMEM((rows, coeffs), F32),
            pltpu.VMEM(m2l.shape, BF16),
            pltpu.VMEM((tiles, leaves, LANES), F32),
            pltpu.VMEM((leaves, tiles * LANES), F32),
            pltpu.VMEM((2 * coeffs, leaves), BF16),
            pltpu.VMEM(packed.shape, F32),
            pltpu.VMEM((tiles * LANES, 64), BF16),
            pltpu.SemaphoreType.DMA((5,)),
        ],
        compiler_params=params(60),
        name="far_field",
    )(first_leaf, counts, blocks, places, *pieces, upper, m2l, l2l, packed, near, wave, phases, mix, contrast)


def leaf_pieces(own, sub):
    coeffs = own.shape[2]
    box = own.reshape(2, 4, 4, 8, coeffs)
    x_side, y_side = (sub >> 1) & 1, (sub >> 2) & 1
    swap = lambda value, bit: lax.ppermute(value, "sub", [(i, i ^ bit) for i in range(16)])
    mirror = swap(own, 8)
    x_face = swap(lax.dynamic_index_in_dim(box, 3 - 3 * x_side, 2, keepdims=False), 2)
    wider = jnp.concatenate([box, x_face[:, :, None]], axis=2)
    y_face = swap(lax.dynamic_index_in_dim(wider, 3 - 3 * y_side, 1, keepdims=False), 4)
    layers = jnp.concatenate([wider, y_face[:, None]], axis=1).reshape(2, 25, 8, coeffs)
    place = lambda z, xy: (z & 1) + 2 * xy + 8 * (z >> 1)
    ups = [(place(z, xy), place(z + 1, xy)) for z in range(3) for xy in range(4)]
    below = lax.ppermute(layers[1], "sub", ups)
    above = lax.ppermute(layers[0], "sub", [(j, i) for i, j in ups])
    return (own, x_face.reshape(8, 8, coeffs), y_face.reshape(10, 8, coeffs), below, above, mirror)


def shards(points, forces, counts, droplet, contrast, ulist, vlist0, vlist1, vlist2,
           wave, phases, p2m_mix, m2m, m2l, l2l, l2p_mix):
    both = ("grp", "sub")
    leaves = counts.shape[0]
    coeffs = m2l.shape[1]
    devices = lax.axis_size(both)
    device = lax.axis_index(both)
    first = device * leaves
    first_arg = first.astype(jnp.int32).reshape(1)

    ids = (first + jnp.arange(leaves * PTS, dtype=jnp.int32) // PTS).astype(F32)[None, :]
    slots = jnp.concatenate([points, forces, droplet.astype(F32)[None, :], ids], axis=0)

    width = HALO * PTS
    count_row = jnp.repeat(counts, PTS).astype(F32)[None, :]

    def edge(part):
        return jnp.concatenate([slots[0:6, part], count_row[:, part], slots[7:8, part]], axis=0)

    packed, leaf_mult, up = upward_pass(first_arg, counts, slots, wave, phases, p2m_mix, m2m)

    mid, top = leaves // 8, leaves // 64
    upper = lax.all_gather(up, both, axis=0, tiled=True).reshape(-1, 8, coeffs)
    pieces = leaf_pieces(leaf_mult.reshape(mid, 8, coeffs), lax.axis_index("sub"))

    last, head = edge(slice(leaves * PTS - width, None)), edge(slice(0, width))
    last, head, packed = lax.optimization_barrier((last, head, packed))
    right_way = [(i, i + 1) for i in range(devices - 1)]
    left_way = [(i + 1, i) for i in range(devices - 1)]
    left = lax.ppermute(last, both, right_way)
    right = lax.ppermute(head, both, left_way)
    left_counts = left[6].reshape(HALO, PTS)[:, 0].astype(jnp.int32)
    right_counts = right[6].reshape(HALO, PTS)[:, 0].astype(jnp.int32)

    near = near_field(first_arg, counts, left_counts, right_counts, packed, left, right, ulist)

    rows0 = first + jnp.arange(leaves, dtype=jnp.int32)
    rows1 = device * mid + jnp.arange(mid, dtype=jnp.int32)
    rows2 = device * top + jnp.arange(top, dtype=jnp.int32)
    places = jnp.concatenate(
        [
            list_places(vlist0, rows0 >> 3, ROOT_BITS - 1),
            list_places(vlist1, rows1 >> 3, ROOT_BITS - 2),
            jnp.pad(list_places(vlist2, rows2 >> 3, ROOT_BITS - 3), ((0, 8 - top), (0, 0)), constant_values=-1),
        ],
        axis=0,
    )
    of_parents = upper_blocks(device * top + jnp.arange(top, dtype=jnp.int32), ROOT_BITS - 2, devices * top)
    of_tops = upper_blocks((device * top >> 3).reshape(1), ROOT_BITS - 3, devices * top // 8)
    blocks = jnp.concatenate(
        [
            leaf_blocks(),
            (of_parents >> 2) * 5 + (of_parents & 3),
            of_tops * 10 + 4,
        ],
        axis=0,
    )
    return far_field(first_arg, counts, blocks, places, pieces, upper, m2l, l2l, packed, near,
                     wave, phases, l2p_mix, contrast[None, :])


def solution(mesh):
    spread = P(("grp", "sub"))
    rows = P(("grp", "sub"), None)
    columns = P(None, ("grp", "sub"))
    return jax.shard_map(
        shards,
        mesh=mesh,
        in_specs=(
            columns, columns, spread, spread, P(), rows, rows, rows, rows,
            P(), P(), P(), P(), P(), P(), P(),
        ),
        out_specs=columns,
        check_vma=False,
    )
```
